32 devices in a mesh: member: 8 (over y, x, core), region: 4 (over z).
Axes of the slice: x: 2, y: 2, z: 4, core: 2. Of those that a mesh axis runs over, the one named last changes fastest.
Arguments:
- state_prior: bfloat16 [256, 98304], P('member', 'region'), may hold values from -6 to 6
- obs_prior: bfloat16 [256, 8192], P('member', 'region'), may hold values from -6 to 6
- obs_value: float32 [8192], P('region'), may hold values from -12 to 12
- obs_rinv: float32 [8192], P('region'), may hold values from 0.02 to 0.3
- tile_obs: int32 [64, 2048], P('region'), may hold values from 64 to 4031, as said below
- tile_count: int32 [64], P('region'), may hold values from 128 to 2048, as said below
Outputs:
- analysis: bfloat16 [256, 98304], P('member', 'region')
The draws below stay inside these ranges and needn't reach their ends.
Inputs may be any that keep to these rules, and one draw needn't show every extreme that they name: tile_obs[t] holds each widened position from i * 128 + 128 / 2 to i * 128 + 128 / 2 + 2047 exactly once, for tile i of its region. `tile_count`: each region has a tile with all 2048 slots live.
All inputs are finite; a program needn't handle non-finite values.
Results may differ from the reference program's by a relative error of at most 0.0015.
The reference program's roundings to bfloat16 on the way (of `xpert` and `wfull`) count: a program that leaves them out, or rounds other values in their place, can miss the bound.
Values may be sent and summed in bfloat16 or wider, within the bound.
A program may use at most 128 MiB of HBM per device.

```python
import math
import jax
import jax.numpy as jnp
from jax import lax

MEMBERS = 256
OBS_TILE = 128
SLOTS = 2048
ITERS = 4
CELLS = 1536
NT_REG = 16
TILES = 64
OBS_REG = 2048
OBS_ALL = 8192
RIM = 1024
LOC = 512


def draw_tile_obs(key, part):
    keys = jax.random.split(key, TILES)
    orders = jax.vmap(lambda one: jax.random.permutation(one, SLOTS))(keys).astype(jnp.int32)
    local_tile = jnp.arange(TILES, dtype=jnp.int32) % NT_REG
    start = local_tile * OBS_TILE + OBS_TILE // 2
    return (start[:, None] + orders).astype(jnp.int32)


def draw_tile_count(key, part):
    regions = TILES // NT_REG
    centers = jax.random.randint(jax.random.fold_in(key, 11), (regions,), 0, NT_REG)
    noise = jax.random.randint(jax.random.fold_in(key, 12), (TILES,), 0, SLOTS // 16)
    index = jnp.arange(TILES, dtype=jnp.int32)
    dist = jnp.abs(index % NT_REG - centers[index // NT_REG])
    value = SLOTS - SLOTS // 16 * dist + noise * (dist > 0).astype(jnp.int32)
    return jnp.clip(value, SLOTS // 16, SLOTS).astype(jnp.int32)


def block_scale(rng, dims, shards, low, top_value):
    def one(axis_at, shards_of):
        heights = jax.random.uniform(jax.random.fold_in(jax.random.fold_in(rng, 6), axis_at), (shards_of,), jnp.float32, low / len(shards), top_value / len(shards))
        return jnp.repeat(jnp.exp(heights), dims[axis_at] // shards_of).reshape((-1,) + (1,) * (len(dims) - axis_at - 1))

    level = one(*shards[0])
    for cut in shards[1:]:
        level = level * one(*cut)
    return level


def normal_values(stream_key, extent, deviation, reach, cuts=(), kind=jnp.bfloat16):
    entries = deviation * jax.random.normal(stream_key, extent, jnp.float32)
    if cuts:
        entries = entries * block_scale(stream_key, extent, cuts, -0.22, 0.18)
    return jnp.clip(entries, -reach, reach).astype(kind)


def setup_inputs(seed: int = 0) -> dict:
    seeds = jax.random.split(jax.random.key(seed), 7)
    return {
        "state_prior": normal_values(seeds[0], (MEMBERS, TILES * CELLS), 1.0, 6.0, ((0, 8), (1, 4))),
        "obs_prior": normal_values(seeds[1], (MEMBERS, OBS_ALL), 1.0, 6.0, ((0, 8), (1, 4))),
        "obs_value": normal_values(seeds[2], (OBS_ALL,), 2.0, 12.0, ((0, 4),), jnp.float32),
        "obs_rinv": jnp.clip(jnp.exp(math.log(0.3) - 2.7080503 * jax.random.uniform(seeds[3], (OBS_ALL,), jnp.float32) ** block_scale(seeds[3], (OBS_ALL,), ((0, 4),), -0.2, 0.2)), 0.02, 0.3),
        "tile_obs": draw_tile_obs(jax.random.fold_in(seeds[6], 71), 0),
        "tile_count": draw_tile_count(jax.random.fold_in(seeds[6], 71), 0),
    }


def analyse(xb, yb, yobs, rinv, slot_pos, count, center):
    size = xb.shape[0]
    slots = yb.shape[1]
    eye = jnp.eye(size, dtype=jnp.float32)
    xfull = xb.astype(jnp.float32)
    xbar = lax.optimization_barrier(jnp.mean(xfull, axis=0))
    xpert = (xfull - xbar).astype(jnp.bfloat16)
    ysel = yb.astype(jnp.float32)
    ybar = lax.optimization_barrier(jnp.mean(ysel, axis=0))
    ypert = ysel - ybar
    depart = yobs - ybar
    dist = jnp.abs(slot_pos - center).astype(jnp.float32) / LOC
    live = (jnp.arange(slots) < count).astype(jnp.float32)
    weight = live * rinv / (1.0 + dist * dist)
    cweighted = ypert * weight
    amat = (size - 1.0) * eye + jnp.dot(cweighted, ypert.T, precision=lax.Precision.HIGHEST)
    rhs = jnp.dot(cweighted, depart, precision=lax.Precision.HIGHEST)
    factor = jnp.linalg.cholesky(amat)
    inner = lax.linalg.triangular_solve(factor, rhs[:, None], left_side=True, lower=True)
    wmean = lax.linalg.triangular_solve(factor, inner, left_side=True, lower=True, transpose_a=True)[:, 0]
    mmat = amat / (size - 1.0)
    scale = jnp.sqrt(jnp.sum(mmat * mmat))
    yiter = mmat / scale
    ziter = eye
    for step in range(ITERS):
        middle = 1.5 * eye - 0.5 * jnp.dot(ziter, yiter, precision=lax.Precision.HIGHEST)
        yiter = jnp.dot(yiter, middle, precision=lax.Precision.HIGHEST)
        ziter = jnp.dot(middle, ziter, precision=lax.Precision.HIGHEST)
    wfull = (ziter / jnp.sqrt(scale) + wmean[:, None]).astype(jnp.bfloat16)
    result = xbar + jnp.dot(wfull.T.astype(jnp.float32), xpert.astype(jnp.float32), preferred_element_type=jnp.float32)
    return result.astype(jnp.bfloat16)

def reference(state_prior, obs_prior, obs_value, obs_rinv, tile_obs, tile_count):
    prior_pad = jnp.pad(obs_prior, ((0, 0), (RIM, RIM)))
    value_pad = jnp.pad(obs_value, (RIM, RIM))
    rinv_pad = jnp.pad(obs_rinv, (RIM, RIM))

    def one_tile(tile):
        region_base = tile // NT_REG * OBS_REG
        local_tile = tile % NT_REG
        slot_pos = tile_obs[tile]
        where = (slot_pos + region_base).astype(jnp.int32)
        ybl = jnp.take(prior_pad, where, axis=1)
        yobs = jnp.take(value_pad, where)
        rinv = jnp.take(rinv_pad, where)
        xb = lax.dynamic_slice_in_dim(state_prior, (tile * CELLS).astype(jnp.int32), CELLS, 1)
        center = RIM + local_tile * OBS_TILE + OBS_TILE // 2
        return analyse(xb, ybl, yobs, rinv, slot_pos, tile_count[tile], center)
    tiles_out = lax.map(one_tile, jnp.arange(TILES, dtype=jnp.int32))
    return jnp.transpose(tiles_out, (1, 0, 2)).reshape(MEMBERS, TILES * CELLS)
```

```python
import functools

import jax
import jax.numpy as jnp
from jax import lax
from jax.experimental import pallas as pl
from jax.experimental.pallas import tpu as pltpu
from jax.sharding import PartitionSpec as P

OBS_TILE = 128
ITERS = 4
RIM = 1024
LOC = 512
CORES = 2
DOUBLINGS = 13
MESH = pl.DeviceIdType.MESH
F32 = jnp.float32
BF16 = jnp.bfloat16


def split(a):
    high = a.astype(BF16)
    return high, (a - high.astype(F32)).astype(BF16)


def mm(a, b):
    return jnp.dot(a, b, preferred_element_type=F32)


def mm_nt(a, b):
    return lax.dot_general(a, b, (((1,), (1,)), ((), ())), preferred_element_type=F32)


def dot3(a, b):
    (ah, al), (bh, bl) = a, b
    return mm(ah, bh) + (mm(ah, bl) + mm(al, bh))


def kernel(
    sizes,
    state, prior, value, rinv, tobs, tcount,
    out,
    pw, vw, rw, yall, xall, res, uh, ul, ev, wt,
    loc_sem, hs_sem, hr_sem, ys_sem, yr_sem, fs_sem, ss_sem, sr_sem, os_sem, or_sem,
):
    groups, regions, rows, per_dev, cells, obs = sizes
    chips = groups // CORES
    members = groups * rows
    me = lax.axis_index("member")
    reg = lax.axis_index("region")
    chip, core = me // CORES, lax.rem(me, CORES)
    sibling = chip * CORES + (CORES - 1 - core)
    wide = obs + 2 * RIM
    width_chip = wide - (chips - 1) * CORES * per_dev * OBS_TILE
    width = width_chip - per_dev * OBS_TILE
    rim_rows = RIM // 128
    obs_rows = obs // 128
    block = per_dev * cells

    def peer(j):
        return lax.rem(me + j, groups)

    barrier = pltpu.get_barrier_semaphore()
    for j in range(1, groups):
        pl.semaphore_signal(barrier, inc=1, device_id={"member": peer(j)}, device_id_type=MESH)

    @pl.when(reg > 0)
    def _():
        pl.semaphore_signal(barrier, inc=1, device_id={"region": reg - 1}, device_id_type=MESH)

    @pl.when(reg < regions - 1)
    def _():
        pl.semaphore_signal(barrier, inc=1, device_id={"region": reg + 1}, device_id_type=MESH)

    own_copies = [
        pltpu.make_async_copy(prior, pw.at[:, pl.ds(RIM, obs)], loc_sem.at[0]),
        pltpu.make_async_copy(value, vw.at[pl.ds(rim_rows, obs_rows), :], loc_sem.at[1]),
        pltpu.make_async_copy(rinv, rw.at[pl.ds(rim_rows, obs_rows), :], loc_sem.at[2]),
    ]
    for copy in own_copies:
        copy.start()

    def state_copy(p, sem_to, sem_from):
        return pltpu.make_async_remote_copy(
            src_ref=state.at[:, pl.ds(pl.multiple_of(p * block, 128), block)],
            dst_ref=xall.at[pl.ds(pl.multiple_of(me * rows, rows), rows), :],
            send_sem=ss_sem.at[sem_to],
            recv_sem=sr_sem.at[sem_from],
            device_id={"member": p},
            device_id_type=MESH,
        )

    own_state = pltpu.make_async_copy(
        state.at[:, pl.ds(pl.multiple_of(me * block, 128), block)],
        xall.at[pl.ds(pl.multiple_of(me * rows, rows), rows), :],
        loc_sem.at[3],
    )
    own_state.start()

    @pl.when(reg == 0)
    def _():
        pw[:, :RIM] = jnp.zeros((rows, RIM), BF16)
        vw[:rim_rows, :] = jnp.zeros((rim_rows, 128), F32)
        rw[:rim_rows, :] = jnp.zeros((rim_rows, 128), F32)

    @pl.when(reg == regions - 1)
    def _():
        pw[:, RIM + obs :] = jnp.zeros((rows, RIM), BF16)
        vw[rim_rows + obs_rows :, :] = jnp.zeros((rim_rows, 128), F32)
        rw[rim_rows + obs_rows :, :] = jnp.zeros((rim_rows, 128), F32)

    expected = groups - 1 + (reg > 0).astype(jnp.int32) + (reg < regions - 1).astype(jnp.int32)
    pl.semaphore_wait(barrier, expected)

    def halo(side):
        at = reg - 1 if side == 0 else reg + 1
        src, dst = (0, RIM + obs) if side == 0 else (obs - RIM, 0)
        src_row, dst_row = src // 128, dst // 128
        made = []
        for n, (a, b) in enumerate(
            (
                (prior.at[:, pl.ds(src, RIM)], pw.at[:, pl.ds(dst, RIM)]),
                (value.at[pl.ds(src_row, rim_rows), :], vw.at[pl.ds(dst_row, rim_rows), :]),
                (rinv.at[pl.ds(src_row, rim_rows), :], rw.at[pl.ds(dst_row, rim_rows), :]),
            )
        ):
            made.append(
                pltpu.make_async_remote_copy(
                    src_ref=a,
                    dst_ref=b,
                    send_sem=hs_sem.at[3 * side + n],
                    recv_sem=hr_sem.at[3 * side + n],
                    device_id={"region": at},
                    device_id_type=MESH,
                )
            )
        return made

    @pl.when(reg > 0)
    def _():
        for copy in halo(0):
            copy.start()

    @pl.when(reg < regions - 1)
    def _():
        for copy in halo(1):
            copy.start()

    state_copy(sibling, 0, me).start()
    for copy in own_copies:
        copy.wait()

    @pl.when(reg < regions - 1)
    def _():
        for copy in halo(0):
            copy.wait_recv()

    @pl.when(reg > 0)
    def _():
        for copy in halo(1):
            copy.wait_recv()

    def window(c):
        return pw.at[:, pl.ds(pl.multiple_of(c * (CORES * per_dev * OBS_TILE), 128), width_chip)]

    def yrows(m):
        return yall.at[pl.ds(pl.multiple_of(m * rows, rows), rows), :]

    def prior_copy(src, source, to, send_sem):
        return pltpu.make_async_remote_copy(
            src_ref=src,
            dst_ref=yrows(source),
            send_sem=send_sem,
            recv_sem=yr_sem.at[source],
            device_id={"member": to},
            device_id_type=MESH,
        )

    sends = []
    for j in range(1, chips):
        c = lax.rem(chip + j, chips)
        sends.append(prior_copy(window(c), me, c * CORES + core, ys_sem.at[j]))
    sends.append(prior_copy(window(chip), me, sibling, ys_sem.at[0]))
    for copy in sends:
        copy.start()
    own_prior = pltpu.make_async_copy(window(chip), yrows(me), loc_sem.at[0])
    own_prior.start()

    pos0 = me * (per_dev * OBS_TILE)
    nrow = width // 128
    hpad = (nrow + 15) // 16 * 16
    slots = tobs.shape[1]
    first = me * per_dev
    lane = lax.broadcasted_iota(jnp.int32, (1, slots), 1)
    hi_iota = lax.broadcasted_iota(jnp.int32, (hpad, slots), 0)
    lo_iota = lax.broadcasted_iota(jnp.int32, (128, slots), 0)
    base = per_dev * me
    value_row = jnp.concatenate([vw[pl.ds(base + h, 1), :] for h in range(nrow)], axis=1)
    rinv_row = jnp.concatenate([rw[pl.ds(base + h, 1), :] for h in range(nrow)], axis=1)
    place = lax.broadcasted_iota(jnp.int32, (1, width), 1)
    weights = []
    for t in range(per_dev):
        rel = tobs[pl.ds(first + t, 1), :] - pos0
        live = lane < tcount[first + t]
        hi = jnp.where(live, rel // 128, -1)
        lo = lax.rem(rel, 128)
        one_hi = jnp.where(hi_iota == hi, 1.0, 0.0).astype(BF16)
        one_lo = jnp.where(lo_iota == lo, 1.0, 0.0).astype(BF16)
        grid = mm_nt(one_hi, one_lo)
        mask = jnp.concatenate([grid[h : h + 1, :] for h in range(nrow)], axis=1)
        dist = jnp.abs(place - (RIM + t * OBS_TILE + OBS_TILE // 2)).astype(F32) / LOC
        weights.append(jnp.sqrt(mask * rinv_row / (1.0 + dist * dist)))

    for j in range(1, chips):
        c = lax.rem(chip + j, chips)
        source = c * CORES + core
        prior_copy(yrows(source), source, sibling, fs_sem.at[j]).wait_recv()
        prior_copy(yrows(source), source, sibling, fs_sem.at[j]).start()
    for copy in sends:
        copy.wait_send()
    for j in range(1, groups):
        p = peer(j)

        @pl.when(p != sibling)
        def _():
            state_copy(p, j, me).start()

    for j in range(chips):
        c = lax.rem(chip + j, chips)
        source = c * CORES + (CORES - 1 - core)
        prior_copy(yrows(source), source, sibling, fs_sem.at[0]).wait_recv()
    own_prior.wait()

    offset = core * (per_dev * OBS_TILE)
    chunk = 256
    sums = [jnp.zeros((members, 128), F32) for _ in range(per_dev)]
    for k in range(width // chunk):
        y = yall[:, pl.ds(pl.multiple_of(offset + k * chunk, 128), chunk)].astype(F32)
        ybar = jnp.sum(y, axis=0, keepdims=True) * (1.0 / members)
        pert = y - ybar
        dep = value_row[:, k * chunk : (k + 1) * chunk] - ybar
        for t in range(per_dev):
            root = weights[t][:, k * chunk : (k + 1) * chunk]
            u = pert * root
            high, low = split(u)
            uh[t, :, k * chunk : (k + 1) * chunk] = high
            ul[t, :, k * chunk : (k + 1) * chunk] = low
            v = u * (root * dep)
            for q in range(chunk // 128):
                sums[t] = sums[t] + v[:, q * 128 : (q + 1) * 128]

    row_i = lax.broadcasted_iota(jnp.int32, (members, members), 0)
    col_i = lax.broadcasted_iota(jnp.int32, (members, members), 1)
    eye = jnp.where(row_i == col_i, 1.0, 0.0).astype(F32)
    scales, zs = [], []
    for t in range(per_dev):
        cross = mm_nt(uh[t], ul[t])
        amat = (members - 1.0) * eye + mm_nt(uh[t], uh[t]) + (cross + cross.T)
        mmat = amat * (1.0 / (members - 1.0))
        scale = jnp.sqrt(jnp.sum(jnp.sum(mmat * mmat, axis=0, keepdims=True), axis=1, keepdims=True))
        y = mmat / scale
        m = 1.5 * eye - 0.5 * y
        z = m
        zp, yp, mp = split(z), split(y), split(m)
        for step in range(1, ITERS + 1):
            yp = split(dot3(yp, mp))
            if step > 1:
                z = dot3(mp, zp)
                zp = split(z)
            p = dot3(zp, yp)
            if step < ITERS:
                mp = split(1.5 * eye - 0.5 * p)
        rhs = jnp.broadcast_to(jnp.sum(sums[t], axis=1, keepdims=True), (members, 128))
        ev[t, :, :members] = eye - p
        ev[t, :, members:] = dot3(zp, split(rhs))
        scales.append(scale)
        zs.append((z, zp))

    def doubling(step, carry):
        for t in range(per_dev):
            e = split(ev[t, :, :members])
            v = ev[t, :, members:]
            ev[t, :, members:] = v + dot3(e, split(v))
            ev[t, :, :members] = dot3(e, e)
        return carry

    lax.fori_loop(0, DOUBLINGS, doubling, 0)
    for t in range(per_dev):
        z, zp = zs[t]
        wmean = dot3(zp, split(ev[t, :, members:])) / (scales[t] * (members - 1.0))
        wide_mean = jnp.concatenate([wmean] * (members // 128), axis=1)
        wt[t] = (z / jnp.sqrt(scales[t]) + wide_mean).T.astype(BF16)

    own_state.wait()
    for j in range(1, groups):
        p = peer(j)
        state_copy(p, j, p).wait_recv()

    def result_copy(p, j, t, sem_from):
        return pltpu.make_async_remote_copy(
            src_ref=res.at[pl.ds(pl.multiple_of(p * rows, rows), rows), pl.ds(t * cells, cells)],
            dst_ref=out.at[:, pl.ds(pl.multiple_of(me * block + t * cells, 128), cells)],
            send_sem=os_sem.at[j, t],
            recv_sem=or_sem.at[sem_from, t],
            device_id={"member": p},
            device_id_type=MESH,
        )

    def own_result(t):
        return pltpu.make_async_copy(
            res.at[pl.ds(pl.multiple_of(me * rows, rows), rows), pl.ds(t * cells, cells)],
            out.at[:, pl.ds(pl.multiple_of(me * block + t * cells, 128), cells)],
            loc_sem.at[1 + t],
        )

    for t in range(per_dev):

        def columns(n, carry):
            at = pl.ds(pl.multiple_of(t * cells + n * chunk, 128), chunk)
            x = xall[:, at].astype(F32)
            xbar = jnp.sum(x, axis=0, keepdims=True) * (1.0 / members)
            pert = (x - xbar).astype(BF16)
            res[:, at] = (xbar + mm(wt[t], pert)).astype(BF16)
            return carry

        lax.fori_loop(0, cells // chunk, columns, 0)
        for j in range(1, groups):
            result_copy(peer(j), j, t, me).start()
        own_result(t).start()

    for t in range(per_dev):
        own_result(t).wait()
        for j in range(1, groups):
            result_copy(peer(j), j, t, me).wait_send()
        for j in range(1, groups):
            p = peer(j)
            result_copy(p, j, t, p).wait_recv()
    for j in range(1, groups):
        p = peer(j)

        @pl.when(p != sibling)
        def _():
            state_copy(p, j, me).wait_send()

    state_copy(sibling, 0, me).wait_send()
    for j in range(1, chips):
        c = lax.rem(chip + j, chips)
        source = c * CORES + core
        prior_copy(yrows(source), source, sibling, fs_sem.at[j]).wait_send()

    @pl.when(reg > 0)
    def _():
        for copy in halo(0):
            copy.wait_send()

    @pl.when(reg < regions - 1)
    def _():
        for copy in halo(1):
            copy.wait_send()


def body(groups, regions, state_prior, obs_prior, obs_value, obs_rinv, tile_obs, tile_count):
    rows = state_prior.shape[0]
    tiles = tile_obs.shape[0]
    per_dev = tiles // groups
    cells = state_prior.shape[1] // tiles
    obs = obs_prior.shape[1]
    members = groups * rows
    chips = groups // CORES
    width_chip = obs + 2 * RIM - (chips - 1) * CORES * per_dev * OBS_TILE
    width = width_chip - per_dev * OBS_TILE
    sizes = (groups, regions, rows, per_dev, cells, obs)
    dma = pltpu.SemaphoreType.DMA
    return pl.pallas_call(
        functools.partial(kernel, sizes),
        out_shape=jax.ShapeDtypeStruct(state_prior.shape, state_prior.dtype),
        in_specs=[pl.BlockSpec(memory_space=pl.ANY)] * 4
        + [pl.BlockSpec(memory_space=pltpu.VMEM), pl.BlockSpec(memory_space=pltpu.SMEM)],
        out_specs=pl.BlockSpec(memory_space=pl.ANY),
        scratch_shapes=[
            pltpu.VMEM((rows, obs + 2 * RIM), BF16),
            pltpu.VMEM(((obs + 2 * RIM) // 128, 128), F32),
            pltpu.VMEM(((obs + 2 * RIM) // 128, 128), F32),
            pltpu.VMEM((members, width_chip), BF16),
            pltpu.VMEM((members, per_dev * cells), BF16),
            pltpu.VMEM((members, per_dev * cells), BF16),
            pltpu.VMEM((per_dev, members, width), BF16),
            pltpu.VMEM((per_dev, members, width), BF16),
            pltpu.VMEM((per_dev, members, members + 128), F32),
            pltpu.VMEM((per_dev, members, members), BF16),
            dma((4,)),
            dma((6,)),
            dma((6,)),
            dma((chips,)),
            dma((groups,)),
            dma((chips,)),
            dma((groups,)),
            dma((groups,)),
            dma((groups, per_dev)),
            dma((groups, per_dev)),
        ],
        compiler_params=pltpu.CompilerParams(
            collective_id=0, has_side_effects=True, vmem_limit_bytes=40 * 1024 * 1024
        ),
        cost_estimate=pl.CostEstimate(flops=4_000_000_000, bytes_accessed=8_000_000, transcendentals=0),
    )(
        state_prior,
        obs_prior,
        obs_value.reshape(-1, 128),
        obs_rinv.reshape(-1, 128),
        tile_obs,
        tile_count,
    )


def solution(mesh):
    placed = (
        P("member", "region"),
        P("member", "region"),
        P("region"),
        P("region"),
        P("region", None),
        P("region"),
    )
    return jax.shard_map(
        functools.partial(body, mesh.shape["member"], mesh.shape["region"]),
        mesh=mesh,
        in_specs=placed,
        out_specs=P("member", "region"),
        check_vma=False,
    )
```

```python
import functools

import jax
import jax.numpy as jnp
import numpy as np
from jax import lax
from jax.experimental import pallas as pl
from jax.experimental.pallas import tpu as pltpu
from jax.sharding import PartitionSpec as P

OBS_TILE = 128
ITERS = 4
RIM = 1024
LOC = 512
CORES = 2
VALUE_MAX = 6.0
RINV_MAX = 0.3
SLOTS_HALF = 1024
MESH = pl.DeviceIdType.MESH
F32 = jnp.float32
BF16 = jnp.bfloat16


def split(a):
    high = a.astype(BF16)
    return high, (a - high.astype(F32)).astype(BF16)


def mm(a, b):
    return jnp.dot(a, b, preferred_element_type=F32)


def mm_nt(a, b):
    return lax.dot_general(a, b, (((1,), (1,)), ((), ())), preferred_element_type=F32)


def dot3(a, b):
    (ah, al), (bh, bl) = a, b
    return mm(jnp.concatenate([ah, ah, al], axis=1), jnp.concatenate([bh, bl, bh], axis=0))


def factors(members):
    apart = np.arange(-SLOTS_HALF, SLOTS_HALF) / LOC
    trace = RINV_MAX * np.sum(1.0 / (1.0 + apart * apart)) * members * VALUE_MAX**2
    low = 0.9 * (members - 1.0) / ((members - 1.0) * np.sqrt(members) + trace)
    scales = []
    while True:
        scales.append(float(2.0 / (1.0 + low)))
        rest = ((1.0 - low) / (1.0 + low)) ** 2
        if rest < 1e-7:
            return scales
        low = 1.0 - rest


def kernel(
    sizes,
    state, prior, value, rinv, tobs, tcount,
    out,
    pw, vw, rw, tv, ts, yall, xall, res, uh, ul, wt,
    loc_sem, hs_sem, hr_sem, ys_sem, yr_sem, fs_sem, ss_sem, sr_sem, os_sem, or_sem,
):
    groups, regions, rows, per_dev, cells, obs = sizes
    chips = groups // CORES
    members = groups * rows
    me = lax.axis_index("member")
    reg = lax.axis_index("region")
    chip, core = me // CORES, lax.rem(me, CORES)
    sibling = chip * CORES + (CORES - 1 - core)
    wide = obs + 2 * RIM
    width_chip = wide - (chips - 1) * CORES * per_dev * OBS_TILE
    width = width_chip - per_dev * OBS_TILE
    rim_rows = RIM // 128
    obs_rows = obs // 128
    block = per_dev * cells

    def peer(j):
        return lax.rem(me + j, groups)

    barrier = pltpu.get_barrier_semaphore()
    for j in range(1, groups):
        pl.semaphore_signal(barrier, inc=1, device_id={"member": peer(j)}, device_id_type=MESH)

    @pl.when(reg > 0)
    def _():
        pl.semaphore_signal(barrier, inc=1, device_id={"region": reg - 1}, device_id_type=MESH)

    @pl.when(reg < regions - 1)
    def _():
        pl.semaphore_signal(barrier, inc=1, device_id={"region": reg + 1}, device_id_type=MESH)

    own_copies = [
        pltpu.make_async_copy(prior, pw.at[:, pl.ds(RIM, obs)], loc_sem.at[0]),
        pltpu.make_async_copy(value, vw.at[pl.ds(rim_rows, obs_rows), :], loc_sem.at[1]),
        pltpu.make_async_copy(rinv, rw.at[pl.ds(rim_rows, obs_rows), :], loc_sem.at[2]),
        pltpu.make_async_copy(tobs, tv, loc_sem.at[4]),
        pltpu.make_async_copy(tcount, ts, loc_sem.at[5]),
    ]
    for copy in own_copies:
        copy.start()

    def state_copy(p, j, t, source):
        return pltpu.make_async_remote_copy(
            src_ref=state.at[:, pl.ds(pl.multiple_of(p * block + t * cells, 128), cells)],
            dst_ref=xall.at[pl.ds(pl.multiple_of(me * rows, rows), rows), pl.ds(t * cells, cells)],
            send_sem=ss_sem.at[j, t],
            recv_sem=sr_sem.at[source, t],
            device_id={"member": p},
            device_id_type=MESH,
        )

    def across(j):
        return lax.rem(chip + j, chips) * CORES + core, CORES * j

    own_state = pltpu.make_async_copy(
        state.at[:, pl.ds(pl.multiple_of(me * block, 128), block)],
        xall.at[pl.ds(pl.multiple_of(me * rows, rows), rows), :],
        loc_sem.at[3],
    )
    own_state.start()

    @pl.when(reg == 0)
    def _():
        pw[:, :RIM] = jnp.zeros((rows, RIM), BF16)
        vw[:rim_rows, :] = jnp.zeros((rim_rows, 128), F32)
        rw[:rim_rows, :] = jnp.zeros((rim_rows, 128), F32)

    @pl.when(reg == regions - 1)
    def _():
        pw[:, RIM + obs :] = jnp.zeros((rows, RIM), BF16)
        vw[rim_rows + obs_rows :, :] = jnp.zeros((rim_rows, 128), F32)
        rw[rim_rows + obs_rows :, :] = jnp.zeros((rim_rows, 128), F32)

    expected = groups - 1 + (reg > 0).astype(jnp.int32) + (reg < regions - 1).astype(jnp.int32)
    pl.semaphore_wait(barrier, expected)

    def halo(side):
        at = reg - 1 if side == 0 else reg + 1
        src, dst = (0, RIM + obs) if side == 0 else (obs - RIM, 0)
        src_row, dst_row = src // 128, dst // 128
        made = []
        for n, (a, b) in enumerate(
            (
                (prior.at[:, pl.ds(src, RIM)], pw.at[:, pl.ds(dst, RIM)]),
                (value.at[pl.ds(src_row, rim_rows), :], vw.at[pl.ds(dst_row, rim_rows), :]),
                (rinv.at[pl.ds(src_row, rim_rows), :], rw.at[pl.ds(dst_row, rim_rows), :]),
            )
        ):
            made.append(
                pltpu.make_async_remote_copy(
                    src_ref=a,
                    dst_ref=b,
                    send_sem=hs_sem.at[3 * side + n],
                    recv_sem=hr_sem.at[3 * side + n],
                    device_id={"region": at},
                    device_id_type=MESH,
                )
            )
        return made

    @pl.when(reg > 0)
    def _():
        for copy in halo(0):
            copy.start()

    @pl.when(reg < regions - 1)
    def _():
        for copy in halo(1):
            copy.start()

    for t in range(per_dev):
        state_copy(sibling, 0, t, me).start()
    for j in range(1, chips):
        p, far = across(j)
        state_copy(p, far, 0, me).start()
    for copy in own_copies:
        copy.wait()

    @pl.when(reg < regions - 1)
    def _():
        for copy in halo(0):
            copy.wait_recv()

    @pl.when(reg > 0)
    def _():
        for copy in halo(1):
            copy.wait_recv()

    def window(c):
        return pw.at[:, pl.ds(pl.multiple_of(c * (CORES * per_dev * OBS_TILE), 128), width_chip)]

    def yrows(m):
        return yall.at[pl.ds(pl.multiple_of(m * rows, rows), rows), :]

    def prior_copy(src, source, to, send_sem):
        return pltpu.make_async_remote_copy(
            src_ref=src,
            dst_ref=yrows(source),
            send_sem=send_sem,
            recv_sem=yr_sem.at[source],
            device_id={"member": to},
            device_id_type=MESH,
        )

    sends = []
    for j in range(1, chips):
        c = lax.rem(chip + j, chips)
        sends.append(prior_copy(window(c), me, c * CORES + core, ys_sem.at[j]))
    sends.append(prior_copy(window(chip), me, sibling, ys_sem.at[0]))
    for copy in sends:
        copy.start()
    own_prior = pltpu.make_async_copy(window(chip), yrows(me), loc_sem.at[0])
    own_prior.start()

    pos0 = me * (per_dev * OBS_TILE)
    nrow = width // 128
    hpad = (nrow + 15) // 16 * 16
    slots = tobs.shape[1]
    first = me * per_dev
    lane = lax.broadcasted_iota(jnp.int32, (1, slots), 1)
    hi_iota = lax.broadcasted_iota(jnp.int32, (hpad, slots), 0)
    lo_iota = lax.broadcasted_iota(jnp.int32, (128, slots), 0)
    base = per_dev * me
    value_row = jnp.concatenate([vw[pl.ds(base + h, 1), :] for h in range(nrow)], axis=1)
    rinv_row = jnp.concatenate([rw[pl.ds(base + h, 1), :] for h in range(nrow)], axis=1)
    place = lax.broadcasted_iota(jnp.int32, (1, width), 1)
    weights = []
    for t in range(per_dev):
        rel = tv[pl.ds(first + t, 1), :] - pos0
        live = lane < ts[first + t]
        hi = jnp.where(live, rel // 128, -1)
        lo = lax.rem(rel, 128)
        one_hi = jnp.where(hi_iota == hi, 1.0, 0.0).astype(BF16)
        one_lo = jnp.where(lo_iota == lo, 1.0, 0.0).astype(BF16)
        grid = mm_nt(one_hi, one_lo)
        mask = jnp.concatenate([grid[h : h + 1, :] for h in range(nrow)], axis=1)
        dist = jnp.abs(place - (RIM + t * OBS_TILE + OBS_TILE // 2)).astype(F32) / LOC
        weights.append(jnp.sqrt(mask * rinv_row / (1.0 + dist * dist)))

    for j in range(1, chips):
        c = lax.rem(chip + j, chips)
        source = c * CORES + core
        prior_copy(yrows(source), source, sibling, fs_sem.at[j]).wait_recv()
        prior_copy(yrows(source), source, sibling, fs_sem.at[j]).start()
    for copy in sends:
        copy.wait_send()
    def other(j):
        return lax.rem(chip + j, chips) * CORES + (CORES - 1 - core), CORES * j + 1

    for j in range(1, chips):
        p, far = other(j)
        state_copy(p, far, 0, me).start()
    for t in range(1, per_dev):
        for j in range(1, chips):
            for p, far in (across(j), other(j)):
                state_copy(p, far, t, me).start()

    for j in range(chips):
        c = lax.rem(chip + j, chips)
        source = c * CORES + (CORES - 1 - core)
        prior_copy(yrows(source), source, sibling, fs_sem.at[0]).wait_recv()
    own_prior.wait()

    offset = core * (per_dev * OBS_TILE)
    chunk = 256
    for k in range(width // chunk):
        at = slice(k * chunk, (k + 1) * chunk)
        y = yall[:, pl.ds(pl.multiple_of(offset + k * chunk, 128), chunk)].astype(F32)
        ybar = jnp.sum(y, axis=0, keepdims=True) * (1.0 / members)
        pert = y - ybar
        dep = value_row[:, at] - ybar
        for t in range(per_dev):
            root = weights[t][:, at]
            high, low = split(pert * root)
            uh[t, :members, at] = high
            ul[t, :, at] = low
            scaled = jnp.broadcast_to(root * dep, (8, chunk))
            rough = scaled.astype(BF16).astype(F32)
            uh[t, members:, at] = jnp.concatenate([rough, scaled - rough], axis=0).astype(BF16)

    row_i = lax.broadcasted_iota(jnp.int32, (members, members), 0)
    col_i = lax.broadcasted_iota(jnp.int32, (members, members), 1)
    eye = jnp.where(row_i == col_i, 1.0, 0.0).astype(F32)
    tiles = range(per_dev)
    cs = factors(members)
    scales, ps, es, vs = [], [], [], []
    main = [mm_nt(uh[t], uh[t, :members, :]) for t in tiles]
    cross = [mm_nt(uh[t], ul[t]) for t in tiles]
    for t in tiles:
        half = cross[t][:members]
        amat = (members - 1.0) * eye + main[t][:members] + (half + half.T)
        mmat = amat * (1.0 / (members - 1.0))
        scale = jnp.sqrt(jnp.sum(jnp.sum(mmat * mmat, axis=0, keepdims=True), axis=1, keepdims=True))
        rhs = main[t][members : members + 1] + main[t][members + 8 : members + 9] + cross[t][members : members + 1]
        scales.append(scale)
        ps.append(mmat / scale)
        vs.append(jnp.broadcast_to(rhs * (float(np.prod(cs)) / (members - 1.0)) / scale, (16, members)))
        es.append(eye - cs[0] * ps[t])

    zs = [1.5 * eye - 0.5 * ps[t] for t in tiles]
    squares = [None for t in tiles]
    for level in range(max(len(cs), 2 * ITERS)):
        for t in tiles:
            if level < len(cs) - 1:
                e = split(es[t])
                v = split(vs[t])
                both = dot3(tuple(jnp.concatenate(x, axis=0) for x in zip(e, v)), e)
                vs[t] = vs[t] + both[members:]
                es[t] = (1.0 - cs[level + 1]) * eye + cs[level + 1] * both[:members]
            elif level == len(cs) - 1:
                vs[t] = vs[t] + dot3(split(vs[t]), split(es[t]))
            if level < 2 * ITERS - 2:
                if level % 2 == 0:
                    p = split(ps[t])
                    squares[t] = dot3(p, p)
                else:
                    ps[t] = 2.25 * ps[t] + dot3(split(squares[t]), split(0.25 * ps[t] - 1.5 * eye))
            if level >= 2 and level % 2 == 0 and level <= 2 * ITERS - 2:
                zs[t] = dot3(split(zs[t]), split(1.5 * eye - 0.5 * ps[t]))
    for t in tiles:
        wt[t] = (zs[t] / jnp.sqrt(scales[t]) + vs[t][:1]).astype(BF16)

    own_state.wait()

    def result_copy(p, j, t, sem_from):
        return pltpu.make_async_remote_copy(
            src_ref=res.at[pl.ds(pl.multiple_of(p * rows, rows), rows), pl.ds(t * cells, cells)],
            dst_ref=out.at[:, pl.ds(pl.multiple_of(me * block + t * cells, 128), cells)],
            send_sem=os_sem.at[j, t],
            recv_sem=or_sem.at[sem_from, t],
            device_id={"member": p},
            device_id_type=MESH,
        )

    def own_result(t):
        return pltpu.make_async_copy(
            res.at[pl.ds(pl.multiple_of(me * rows, rows), rows), pl.ds(t * cells, cells)],
            out.at[:, pl.ds(pl.multiple_of(me * block + t * cells, 128), cells)],
            loc_sem.at[1 + t],
        )

    for t in range(per_dev):
        for j in range(1, groups):
            p = peer(j)
            state_copy(p, j, t, p).wait_recv()

        def columns(n, carry):
            at = pl.ds(pl.multiple_of(t * cells + n * chunk, 128), chunk)
            x = xall[:, at].astype(F32)
            xbar = jnp.sum(x, axis=0, keepdims=True) * (1.0 / members)
            pert = (x - xbar).astype(BF16)
            res[:, at] = (xbar + mm(wt[t], pert)).astype(BF16)
            return carry

        lax.fori_loop(0, cells // chunk, columns, 0)
        for j in range(1, groups):
            result_copy(peer(j), j, t, me).start()
        own_result(t).start()

    for t in range(per_dev):
        own_result(t).wait()
        for j in range(1, groups):
            result_copy(peer(j), j, t, me).wait_send()
        for j in range(1, groups):
            p = peer(j)
            result_copy(p, j, t, p).wait_recv()
    for t in range(per_dev):
        state_copy(sibling, 0, t, me).wait_send()
        for j in range(1, chips):
            for p, far in (across(j), other(j)):
                state_copy(p, far, t, me).wait_send()
    for j in range(1, chips):
        c = lax.rem(chip + j, chips)
        source = c * CORES + core
        prior_copy(yrows(source), source, sibling, fs_sem.at[j]).wait_send()

    @pl.when(reg > 0)
    def _():
        for copy in halo(0):
            copy.wait_send()

    @pl.when(reg < regions - 1)
    def _():
        for copy in halo(1):
            copy.wait_send()


def body(groups, regions, state_prior, obs_prior, obs_value, obs_rinv, tile_obs, tile_count):
    rows = state_prior.shape[0]
    tiles = tile_obs.shape[0]
    per_dev = tiles // groups
    cells = state_prior.shape[1] // tiles
    obs = obs_prior.shape[1]
    members = groups * rows
    chips = groups // CORES
    width_chip = obs + 2 * RIM - (chips - 1) * CORES * per_dev * OBS_TILE
    width = width_chip - per_dev * OBS_TILE
    sizes = (groups, regions, rows, per_dev, cells, obs)
    dma = pltpu.SemaphoreType.DMA
    return pl.pallas_call(
        functools.partial(kernel, sizes),
        out_shape=jax.ShapeDtypeStruct(state_prior.shape, state_prior.dtype),
        in_specs=[pl.BlockSpec(memory_space=pl.ANY)] * 6,
        out_specs=pl.BlockSpec(memory_space=pl.ANY),
        scratch_shapes=[
            pltpu.VMEM((rows, obs + 2 * RIM), BF16),
            pltpu.VMEM(((obs + 2 * RIM) // 128, 128), F32),
            pltpu.VMEM(((obs + 2 * RIM) // 128, 128), F32),
            pltpu.VMEM(tile_obs.shape, jnp.int32),
            pltpu.SMEM(tile_count.shape, jnp.int32),
            pltpu.VMEM((members, width_chip), BF16),
            pltpu.VMEM((members, per_dev * cells), BF16),
            pltpu.VMEM((members, per_dev * cells), BF16),
            pltpu.VMEM((per_dev, members + 16, width), BF16),
            pltpu.VMEM((per_dev, members, width), BF16),
            pltpu.VMEM((per_dev, members, members), BF16),
            dma((6,)),
            dma((6,)),
            dma((6,)),
            dma((chips,)),
            dma((groups,)),
            dma((chips,)),
            dma((groups, per_dev)),
            dma((groups, per_dev)),
            dma((groups, per_dev)),
            dma((groups, per_dev)),
        ],
        compiler_params=pltpu.CompilerParams(
            collective_id=0, has_side_effects=True, vmem_limit_bytes=62 * 1024 * 1024
        ),
        cost_estimate=pl.CostEstimate(flops=4_000_000_000, bytes_accessed=8_000_000, transcendentals=0),
    )(
        state_prior,
        obs_prior,
        obs_value.reshape(-1, 128),
        obs_rinv.reshape(-1, 128),
        tile_obs,
        tile_count,
    )


def solution(mesh):
    placed = (
        P("member", "region"),
        P("member", "region"),
        P("region"),
        P("region"),
        P("region", None),
        P("region"),
    )
    return jax.shard_map(
        functools.partial(body, mesh.shape["member"], mesh.shape["region"]),
        mesh=mesh,
        in_specs=placed,
        out_specs=P("member", "region"),
        check_vma=False,
    )
```

```python
import functools

import jax
import jax.numpy as jnp
import numpy as np
from jax import lax
from jax.experimental import pallas as pl
from jax.experimental.pallas import tpu as pltpu
from jax.sharding import PartitionSpec as P

OBS_TILE = 128
ITERS = 4
RIM = 1024
LOC = 512
CORES = 2
VALUE_MAX = 6.0
RINV_MAX = 0.3
SLOTS_HALF = 1024
PIECE = 512
MESH = pl.DeviceIdType.MESH
F32 = jnp.float32
BF16 = jnp.bfloat16


def split(a):
    high = a.astype(BF16)
    return high, (a - high.astype(F32)).astype(BF16)


def mm(a, b):
    return jnp.dot(a, b, preferred_element_type=F32)


def mm_nt(a, b):
    return lax.dot_general(a, b, (((1,), (1,)), ((), ())), preferred_element_type=F32)


def dot3(a, b):
    (ah, al), (bh, bl) = a, b
    return mm(jnp.concatenate([ah, ah, al], axis=1), jnp.concatenate([bh, bl, bh], axis=0))


def factors(members):
    apart = np.arange(-SLOTS_HALF, SLOTS_HALF) / LOC
    trace = RINV_MAX * np.sum(1.0 / (1.0 + apart * apart)) * members * VALUE_MAX**2
    low = 0.9 * (members - 1.0) / ((members - 1.0) * np.sqrt(members) + trace)
    scales = []
    while True:
        scales.append(float(2.0 / (1.0 + low)))
        rest = ((1.0 - low) / (1.0 + low)) ** 2
        if rest < 1e-7:
            return scales
        low = 1.0 - rest


def kernel(
    sizes,
    state, prior, value, rinv, tobs, tcount,
    out,
    pw, vw, rw, tv, ts, roots, values, yall, xall, res, uh, ul, wt,
    loc_sem, own_sem, hs_sem, hr_sem, ys_sem, yr_sem, fs_sem, ss_sem, sr_sem, os_sem, or_sem,
):
    groups, regions, rows, per_dev, cells, obs = sizes
    chips = groups // CORES
    members = groups * rows
    me = lax.axis_index("member")
    reg = lax.axis_index("region")
    chip, core = me // CORES, lax.rem(me, CORES)
    sibling = chip * CORES + (CORES - 1 - core)
    wide = obs + 2 * RIM
    width_chip = wide - (chips - 1) * CORES * per_dev * OBS_TILE
    half_width = width_chip // 2
    rim_rows = RIM // 128
    obs_rows = obs // 128
    block = per_dev * cells

    def peer(j):
        return lax.rem(me + j, groups)

    barrier = pltpu.get_barrier_semaphore()
    for j in range(1, groups):
        pl.semaphore_signal(barrier, inc=1, device_id={"member": peer(j)}, device_id_type=MESH)

    @pl.when(reg > 0)
    def _():
        pl.semaphore_signal(barrier, inc=1, device_id={"region": reg - 1}, device_id_type=MESH)

    @pl.when(reg < regions - 1)
    def _():
        pl.semaphore_signal(barrier, inc=1, device_id={"region": reg + 1}, device_id_type=MESH)

    own_copies = [
        pltpu.make_async_copy(prior, pw.at[:, pl.ds(RIM, obs)], loc_sem.at[0]),
        pltpu.make_async_copy(value, vw.at[pl.ds(rim_rows, obs_rows), :], loc_sem.at[1]),
        pltpu.make_async_copy(rinv, rw.at[pl.ds(rim_rows, obs_rows), :], loc_sem.at[2]),
        pltpu.make_async_copy(tobs, tv, loc_sem.at[4]),
        pltpu.make_async_copy(tcount, ts, loc_sem.at[5]),
    ]
    for copy in own_copies:
        copy.start()

    def state_copy(p, j, t, source):
        return pltpu.make_async_remote_copy(
            src_ref=state.at[:, pl.ds(pl.multiple_of(p * block + t * cells, 128), cells)],
            dst_ref=xall.at[pl.ds(pl.multiple_of(me * rows, rows), rows), pl.ds(t * cells, cells)],
            send_sem=ss_sem.at[j, t],
            recv_sem=sr_sem.at[source, t],
            device_id={"member": p},
            device_id_type=MESH,
        )

    def across(j):
        return lax.rem(chip + j, chips) * CORES + core, CORES * j

    own_state = pltpu.make_async_copy(
        state.at[:, pl.ds(pl.multiple_of(me * block, 128), block)],
        xall.at[pl.ds(pl.multiple_of(me * rows, rows), rows), :],
        loc_sem.at[3],
    )
    own_state.start()

    @pl.when(reg == 0)
    def _():
        pw[:, :RIM] = jnp.zeros((rows, RIM), BF16)
        vw[:rim_rows, :] = jnp.zeros((rim_rows, 128), F32)
        rw[:rim_rows, :] = jnp.zeros((rim_rows, 128), F32)

    @pl.when(reg == regions - 1)
    def _():
        pw[:, RIM + obs :] = jnp.zeros((rows, RIM), BF16)
        vw[rim_rows + obs_rows :, :] = jnp.zeros((rim_rows, 128), F32)
        rw[rim_rows + obs_rows :, :] = jnp.zeros((rim_rows, 128), F32)

    expected = groups - 1 + (reg > 0).astype(jnp.int32) + (reg < regions - 1).astype(jnp.int32)
    pl.semaphore_wait(barrier, expected)

    def halo(side):
        at = reg - 1 if side == 0 else reg + 1
        src, dst = (0, RIM + obs) if side == 0 else (obs - RIM, 0)
        src_row, dst_row = src // 128, dst // 128
        made = []
        for n, (a, b) in enumerate(
            (
                (prior.at[:, pl.ds(src, RIM)], pw.at[:, pl.ds(dst, RIM)]),
                (value.at[pl.ds(src_row, rim_rows), :], vw.at[pl.ds(dst_row, rim_rows), :]),
                (rinv.at[pl.ds(src_row, rim_rows), :], rw.at[pl.ds(dst_row, rim_rows), :]),
            )
        ):
            made.append(
                pltpu.make_async_remote_copy(
                    src_ref=a,
                    dst_ref=b,
                    send_sem=hs_sem.at[3 * side + n],
                    recv_sem=hr_sem.at[3 * side + n],
                    device_id={"region": at},
                    device_id_type=MESH,
                )
            )
        return made

    @pl.when(reg > 0)
    def _():
        for copy in halo(0):
            copy.start()

    @pl.when(reg < regions - 1)
    def _():
        for copy in halo(1):
            copy.start()

    def begin(c, half):
        inner = 1 - (2 * c) // chips
        return (inner if half == 0 else 1 - inner) * half_width

    def window(c, half):
        at = c * (CORES * per_dev * OBS_TILE) + begin(c, half)
        return pw.at[:, pl.ds(pl.multiple_of(at, 128), half_width)]

    def yrows(m, half):
        at = pl.multiple_of(begin(chip, half), 128)
        return yall.at[pl.ds(pl.multiple_of(m * rows, rows), rows), pl.ds(at, half_width)]

    def prior_copy(c, source, to, half, j):
        at = pl.multiple_of(begin(c, half), 128)
        return pltpu.make_async_remote_copy(
            src_ref=window(c, half),
            dst_ref=yall.at[pl.ds(pl.multiple_of(source * rows, rows), rows), pl.ds(at, half_width)],
            send_sem=ys_sem.at[j, half],
            recv_sem=yr_sem.at[source, half],
            device_id={"member": to},
            device_id_type=MESH,
        )

    def forward_copy(source, half, j):
        return pltpu.make_async_remote_copy(
            src_ref=yrows(source, half),
            dst_ref=yrows(source, half),
            send_sem=fs_sem.at[j, half],
            recv_sem=yr_sem.at[source, half],
            device_id={"member": sibling},
            device_id_type=MESH,
        )

    def own_prior(half):
        return pltpu.make_async_copy(window(chip, half), yrows(me, half), loc_sem.at[6 + half])

    def prior_sends(half):
        made = []
        for j in range(1, chips):
            c = lax.rem(chip + j, chips)
            made.append(prior_copy(c, me, c * CORES + core, half, j))
        made.append(prior_copy(chip, me, sibling, half, 0))
        return made

    def forward(half):
        for j in range(1, chips):
            c = lax.rem(chip + j, chips)
            source = c * CORES + core
            forward_copy(source, half, j).wait_recv()
            forward_copy(source, half, j).start()

    def gathered(half):
        own_prior(half).wait()
        for j in range(chips):
            c = lax.rem(chip + j, chips)
            forward_copy(c * CORES + (CORES - 1 - core), half, j).wait_recv()

    def other(j):
        return lax.rem(chip + j, chips) * CORES + (CORES - 1 - core), CORES * j + 1

    def start_state(t):
        for j in range(1, chips):
            for p, far in (across(j), other(j)):
                state_copy(p, far, t, me).start()

    for copy in own_copies:
        copy.wait()
    for copy in prior_sends(0):
        copy.start()
    own_prior(0).start()
    for t in range(per_dev):
        state_copy(sibling, 0, t, me).start()

    @pl.when(reg < regions - 1)
    def _():
        for copy in halo(0):
            copy.wait_recv()

    @pl.when(reg > 0)
    def _():
        for copy in halo(1):
            copy.wait_recv()

    for copy in prior_sends(1):
        copy.start()
    own_prior(1).start()

    pos0 = chip * (CORES * per_dev * OBS_TILE)
    nrow = width_chip // 128
    hpad = (nrow + 15) // 16 * 16
    slots = tobs.shape[1]
    first = me * per_dev
    lane = lax.broadcasted_iota(jnp.int32, (1, slots), 1)
    hi_iota = lax.broadcasted_iota(jnp.int32, (hpad, slots), 0)
    lo_iota = lax.broadcasted_iota(jnp.int32, (128, slots), 0)
    base = chip * (CORES * per_dev * OBS_TILE // 128)
    values[...] = jnp.concatenate([vw[pl.ds(base + h, 1), :] for h in range(nrow)], axis=1)
    rinv_row = jnp.concatenate([rw[pl.ds(base + h, 1), :] for h in range(nrow)], axis=1)
    place = lax.broadcasted_iota(jnp.int32, (1, width_chip), 1)
    centre0 = RIM + OBS_TILE // 2 + core * (per_dev * OBS_TILE)
    for t in range(per_dev):
        rel = tv[pl.ds(first + t, 1), :] - pos0
        live = lane < ts[first + t]
        hi = jnp.where(live, rel // 128, -1)
        lo = lax.rem(rel, 128)
        one_hi = jnp.where(hi_iota == hi, 1.0, 0.0).astype(BF16)
        one_lo = jnp.where(lo_iota == lo, 1.0, 0.0).astype(BF16)
        grid = mm_nt(one_hi, one_lo)
        mask = jnp.concatenate([grid[h : h + 1, :] for h in range(nrow)], axis=1)
        dist = jnp.abs(place - (centre0 + t * OBS_TILE)).astype(F32) / LOC
        roots[t] = jnp.sqrt(mask * rinv_row / (1.0 + dist * dist))

    chunk = 256
    tiles = range(per_dev)

    def perturb(half):
        for k in range(half_width // chunk):
            at = pl.ds(pl.multiple_of(begin(chip, half) + k * chunk, 128), chunk)
            y = yall[:, at].astype(F32)
            ybar = jnp.sum(y, axis=0, keepdims=True) * (1.0 / members)
            pert = y - ybar
            dep = values[:, at] - ybar
            for t in tiles:
                root = roots[t, :, at]
                high, low = split(pert * root)
                uh[t, :members, at] = high
                ul[t, :, at] = low
                scaled = jnp.broadcast_to(root * dep, (8, chunk))
                rough = scaled.astype(BF16).astype(F32)
                uh[t, members:, at] = jnp.concatenate([rough, scaled - rough], axis=0).astype(BF16)

    def products(half):
        at = pl.ds(pl.multiple_of(begin(chip, half), 128), half_width)
        both = [uh[t, :, at] for t in tiles]
        main = [mm_nt(both[t], both[t][:members]) for t in tiles]
        return main, [mm_nt(both[t], ul[t, :, at]) for t in tiles]

    forward(0)
    gathered(0)
    perturb(0)
    for half in range(2):
        for copy in prior_sends(half):
            copy.wait_send()
    start_state(0)
    main, cross = products(0)
    forward(1)
    for t in range(1, per_dev):
        start_state(t)
    gathered(1)
    perturb(1)
    more_main, more_cross = products(1)
    main = [a + b for a, b in zip(main, more_main)]
    cross = [a + b for a, b in zip(cross, more_cross)]

    row_i = lax.broadcasted_iota(jnp.int32, (members, members), 0)
    col_i = lax.broadcasted_iota(jnp.int32, (members, members), 1)
    eye = jnp.where(row_i == col_i, 1.0, 0.0).astype(F32)
    cs = factors(members)
    scales, ps, es, vs = [], [], [], []
    for t in tiles:
        half = cross[t][:members]
        amat = (members - 1.0) * eye + main[t][:members] + (half + half.T)
        mmat = amat * (1.0 / (members - 1.0))
        scale = jnp.sqrt(jnp.sum(jnp.sum(mmat * mmat, axis=0, keepdims=True), axis=1, keepdims=True))
        rhs = main[t][members : members + 1] + main[t][members + 8 : members + 9] + cross[t][members : members + 1]
        scales.append(scale)
        ps.append(mmat / scale)
        vs.append(jnp.broadcast_to(rhs * (float(np.prod(cs)) / (members - 1.0)) / scale, (16, members)))
        es.append(eye - cs[0] * ps[t])

    zs = [1.5 * eye - 0.5 * ps[t] for t in tiles]
    squares = [None for t in tiles]
    for level in range(max(len(cs), 2 * ITERS)):
        for t in tiles:
            if level < len(cs) - 1:
                e = split(es[t])
                v = split(vs[t])
                both = dot3(tuple(jnp.concatenate(x, axis=0) for x in zip(e, v)), e)
                vs[t] = vs[t] + both[members:]
                es[t] = (1.0 - cs[level + 1]) * eye + cs[level + 1] * both[:members]
            elif level == len(cs) - 1:
                vs[t] = vs[t] + dot3(split(vs[t]), split(es[t]))
            if level < 2 * ITERS - 2:
                if level % 2 == 0:
                    p = split(ps[t])
                    squares[t] = dot3(p, p)
                else:
                    ps[t] = 2.25 * ps[t] + dot3(split(squares[t]), split(0.25 * ps[t] - 1.5 * eye))
            if level >= 2 and level % 2 == 0 and level <= 2 * ITERS - 2:
                zs[t] = dot3(split(zs[t]), split(1.5 * eye - 0.5 * ps[t]))
    for t in tiles:
        wt[t] = (zs[t] / jnp.sqrt(scales[t]) + vs[t][:1]).astype(BF16)

    own_state.wait()

    def result_copy(p, j, n, source):
        return pltpu.make_async_remote_copy(
            src_ref=res.at[pl.ds(pl.multiple_of(p * rows, rows), rows), pl.ds(n * PIECE, PIECE)],
            dst_ref=out.at[:, pl.ds(pl.multiple_of(me * block + n * PIECE, 128), PIECE)],
            send_sem=os_sem.at[j, n],
            recv_sem=or_sem.at[source, n],
            device_id={"member": p},
            device_id_type=MESH,
        )

    def own_result(n):
        return pltpu.make_async_copy(
            res.at[pl.ds(pl.multiple_of(me * rows, rows), rows), pl.ds(n * PIECE, PIECE)],
            out.at[:, pl.ds(pl.multiple_of(me * block + n * PIECE, 128), PIECE)],
            own_sem.at[n],
        )

    pieces = block // PIECE
    for n in range(pieces):
        t = n * PIECE // cells
        if n * PIECE % cells == 0:
            for j in range(1, groups):
                p = peer(j)
                state_copy(p, j, t, p).wait_recv()
        for k in range(PIECE // chunk):
            at = slice(n * PIECE + k * chunk, n * PIECE + (k + 1) * chunk)
            x = xall[:, at].astype(F32)
            xbar = jnp.sum(x, axis=0, keepdims=True) * (1.0 / members)
            pert = (x - xbar).astype(BF16)
            res[:, at] = (xbar + mm(wt[t], pert)).astype(BF16)
        for j in range(1, groups):
            result_copy(peer(j), j, n, me).start()
        own_result(n).start()

    for n in range(pieces):
        own_result(n).wait()
        for j in range(1, groups):
            p = peer(j)
            result_copy(p, j, n, p).wait_recv()
        for j in range(1, groups):
            result_copy(peer(j), j, n, me).wait_send()
    for t in range(per_dev):
        state_copy(sibling, 0, t, me).wait_send()
        for j in range(1, chips):
            for p, far in (across(j), other(j)):
                state_copy(p, far, t, me).wait_send()
    for half in range(2):
        for j in range(1, chips):
            c = lax.rem(chip + j, chips)
            forward_copy(c * CORES + core, half, j).wait_send()

    @pl.when(reg > 0)
    def _():
        for copy in halo(0):
            copy.wait_send()

    @pl.when(reg < regions - 1)
    def _():
        for copy in halo(1):
            copy.wait_send()


def body(groups, regions, state_prior, obs_prior, obs_value, obs_rinv, tile_obs, tile_count):
    rows = state_prior.shape[0]
    tiles = tile_obs.shape[0]
    per_dev = tiles // groups
    cells = state_prior.shape[1] // tiles
    obs = obs_prior.shape[1]
    members = groups * rows
    chips = groups // CORES
    width_chip = obs + 2 * RIM - (chips - 1) * CORES * per_dev * OBS_TILE
    pieces = per_dev * cells // PIECE
    sizes = (groups, regions, rows, per_dev, cells, obs)
    dma = pltpu.SemaphoreType.DMA
    return pl.pallas_call(
        functools.partial(kernel, sizes),
        out_shape=jax.ShapeDtypeStruct(state_prior.shape, state_prior.dtype),
        in_specs=[pl.BlockSpec(memory_space=pl.ANY)] * 6,
        out_specs=pl.BlockSpec(memory_space=pl.ANY),
        scratch_shapes=[
            pltpu.VMEM((rows, obs + 2 * RIM), BF16),
            pltpu.VMEM(((obs + 2 * RIM) // 128, 128), F32),
            pltpu.VMEM(((obs + 2 * RIM) // 128, 128), F32),
            pltpu.VMEM(tile_obs.shape, jnp.int32),
            pltpu.SMEM(tile_count.shape, jnp.int32),
            pltpu.VMEM((per_dev, 1, width_chip), F32),
            pltpu.VMEM((1, width_chip), F32),
            pltpu.VMEM((members, width_chip), BF16),
            pltpu.VMEM((members, per_dev * cells), BF16),
            pltpu.VMEM((members, per_dev * cells), BF16),
            pltpu.VMEM((per_dev, members + 16, width_chip), BF16),
            pltpu.VMEM((per_dev, members, width_chip), BF16),
            pltpu.VMEM((per_dev, members, members), BF16),
            dma((8,)),
            dma((pieces,)),
            dma((6,)),
            dma((6,)),
            dma((chips, 2)),
            dma((groups, 2)),
            dma((chips, 2)),
            dma((groups, per_dev)),
            dma((groups, per_dev)),
            dma((groups, pieces)),
            dma((groups, pieces)),
        ],
        compiler_params=pltpu.CompilerParams(
            collective_id=0, has_side_effects=True, vmem_limit_bytes=62 * 1024 * 1024
        ),
        cost_estimate=pl.CostEstimate(flops=4_000_000_000, bytes_accessed=8_000_000, transcendentals=0),
    )(
        state_prior,
        obs_prior,
        obs_value.reshape(-1, 128),
        obs_rinv.reshape(-1, 128),
        tile_obs,
        tile_count,
    )


def solution(mesh):
    placed = (
        P("member", "region"),
        P("member", "region"),
        P("region"),
        P("region"),
        P("region", None),
        P("region"),
    )
    return jax.shard_map(
        functools.partial(body, mesh.shape["member"], mesh.shape["region"]),
        mesh=mesh,
        in_specs=placed,
        out_specs=P("member", "region"),
        check_vma=False,
    )
```

```python
import functools

import jax
import jax.numpy as jnp
import numpy as np
from jax import lax
from jax.experimental import pallas as pl
from jax.experimental.pallas import tpu as pltpu
from jax.sharding import PartitionSpec as P

OBS_TILE = 128
ITERS = 4
RIM = 1024
LOC = 512
CORES = 2
VALUE_MAX = 6.0
RINV_MAX = 0.3
SLOTS_HALF = 1024
PIECE = 512
MESH = pl.DeviceIdType.MESH
F32 = jnp.float32
BF16 = jnp.bfloat16


def split(a):
    high = a.astype(BF16)
    return high, (a - high.astype(F32)).astype(BF16)


def mm(a, b):
    return jnp.dot(a, b, preferred_element_type=F32)


def mm_nt(a, b):
    return lax.dot_general(a, b, (((1,), (1,)), ((), ())), preferred_element_type=F32)


def dot3(a, b):
    (ah, al), (bh, bl) = a, b
    return mm(jnp.concatenate([ah, ah, al], axis=1), jnp.concatenate([bh, bl, bh], axis=0))


def factors(members):
    apart = np.arange(-SLOTS_HALF, SLOTS_HALF) / LOC
    trace = RINV_MAX * np.sum(1.0 / (1.0 + apart * apart)) * members * VALUE_MAX**2
    low = 0.9 * (members - 1.0) / ((members - 1.0) * np.sqrt(members) + trace)
    scales = []
    while True:
        scales.append(float(2.0 / (1.0 + low)))
        rest = ((1.0 - low) / (1.0 + low)) ** 2
        if rest < 1e-7:
            return scales
        low = 1.0 - rest


def kernel(
    sizes,
    state, prior, value, rinv, tobs, tcount,
    out,
    pw, vw, rw, tv, ts, roots, values, yall, xall, res, uh, ul, wt,
    loc_sem, own_sem, hs_sem, hr_sem, ys_sem, yr_sem, fs_sem, ss_sem, sr_sem, os_sem, or_sem,
):
    groups, regions, rows, per_dev, cells, obs = sizes
    chips = groups // CORES
    members = groups * rows
    me = lax.axis_index("member")
    reg = lax.axis_index("region")
    chip, core = me // CORES, lax.rem(me, CORES)
    sibling = chip * CORES + (CORES - 1 - core)
    wide = obs + 2 * RIM
    width_chip = wide - (chips - 1) * CORES * per_dev * OBS_TILE
    half_width = width_chip // 2
    rim_rows = RIM // 128
    obs_rows = obs // 128
    block = per_dev * cells

    def peer(j):
        return lax.rem(me + j, groups)

    barrier = pltpu.get_barrier_semaphore()
    for j in range(1, groups):
        pl.semaphore_signal(barrier, inc=1, device_id={"member": peer(j)}, device_id_type=MESH)

    @pl.when(reg > 0)
    def _():
        pl.semaphore_signal(barrier, inc=1, device_id={"region": reg - 1}, device_id_type=MESH)

    @pl.when(reg < regions - 1)
    def _():
        pl.semaphore_signal(barrier, inc=1, device_id={"region": reg + 1}, device_id_type=MESH)

    own_copies = [
        pltpu.make_async_copy(prior, pw.at[:, pl.ds(RIM, obs)], loc_sem.at[0]),
        pltpu.make_async_copy(value, vw.at[pl.ds(rim_rows, obs_rows), :], loc_sem.at[1]),
        pltpu.make_async_copy(rinv, rw.at[pl.ds(rim_rows, obs_rows), :], loc_sem.at[2]),
        pltpu.make_async_copy(tobs, tv, loc_sem.at[4]),
        pltpu.make_async_copy(tcount, ts, loc_sem.at[5]),
    ]
    for copy in own_copies:
        copy.start()

    def state_copy(p, j, t, source):
        return pltpu.make_async_remote_copy(
            src_ref=state.at[:, pl.ds(pl.multiple_of(p * block + t * cells, 128), cells)],
            dst_ref=xall.at[pl.ds(pl.multiple_of(me * rows, rows), rows), pl.ds(t * cells, cells)],
            send_sem=ss_sem.at[j, t],
            recv_sem=sr_sem.at[source, t],
            device_id={"member": p},
            device_id_type=MESH,
        )

    def across(j):
        return lax.rem(chip + j, chips) * CORES + core, CORES * j

    own_state = pltpu.make_async_copy(
        state.at[:, pl.ds(pl.multiple_of(me * block, 128), block)],
        xall.at[pl.ds(pl.multiple_of(me * rows, rows), rows), :],
        loc_sem.at[3],
    )
    own_state.start()

    @pl.when(reg == 0)
    def _():
        pw[:, :RIM] = jnp.zeros((rows, RIM), BF16)
        vw[:rim_rows, :] = jnp.zeros((rim_rows, 128), F32)
        rw[:rim_rows, :] = jnp.zeros((rim_rows, 128), F32)

    @pl.when(reg == regions - 1)
    def _():
        pw[:, RIM + obs :] = jnp.zeros((rows, RIM), BF16)
        vw[rim_rows + obs_rows :, :] = jnp.zeros((rim_rows, 128), F32)
        rw[rim_rows + obs_rows :, :] = jnp.zeros((rim_rows, 128), F32)

    expected = groups - 1 + (reg > 0).astype(jnp.int32) + (reg < regions - 1).astype(jnp.int32)
    pl.semaphore_wait(barrier, expected)

    def halo(side):
        at = reg - 1 if side == 0 else reg + 1
        src, dst = (0, RIM + obs) if side == 0 else (obs - RIM, 0)
        src_row, dst_row = src // 128, dst // 128
        made = []
        for n, (a, b) in enumerate(
            (
                (prior.at[:, pl.ds(src, RIM)], pw.at[:, pl.ds(dst, RIM)]),
                (value.at[pl.ds(src_row, rim_rows), :], vw.at[pl.ds(dst_row, rim_rows), :]),
                (rinv.at[pl.ds(src_row, rim_rows), :], rw.at[pl.ds(dst_row, rim_rows), :]),
            )
        ):
            made.append(
                pltpu.make_async_remote_copy(
                    src_ref=a,
                    dst_ref=b,
                    send_sem=hs_sem.at[3 * side + n],
                    recv_sem=hr_sem.at[3 * side + n],
                    device_id={"region": at},
                    device_id_type=MESH,
                )
            )
        return made

    @pl.when(reg > 0)
    def _():
        for copy in halo(0):
            copy.start()

    @pl.when(reg < regions - 1)
    def _():
        for copy in halo(1):
            copy.start()

    def begin(c, half):
        inner = 1 - (2 * c) // chips
        return (inner if half == 0 else 1 - inner) * half_width

    def window(c, half):
        at = c * (CORES * per_dev * OBS_TILE) + begin(c, half)
        return pw.at[:, pl.ds(pl.multiple_of(at, 128), half_width)]

    def yrows(m, half):
        at = pl.multiple_of(begin(chip, half), 128)
        return yall.at[pl.ds(pl.multiple_of(m * rows, rows), rows), pl.ds(at, half_width)]

    def prior_copy(c, source, to, half, j):
        at = pl.multiple_of(begin(c, half), 128)
        return pltpu.make_async_remote_copy(
            src_ref=window(c, half),
            dst_ref=yall.at[pl.ds(pl.multiple_of(source * rows, rows), rows), pl.ds(at, half_width)],
            send_sem=ys_sem.at[j, half],
            recv_sem=yr_sem.at[source, half],
            device_id={"member": to},
            device_id_type=MESH,
        )

    def forward_copy(source, half, j):
        return pltpu.make_async_remote_copy(
            src_ref=yrows(source, half),
            dst_ref=yrows(source, half),
            send_sem=fs_sem.at[j, half],
            recv_sem=yr_sem.at[source, half],
            device_id={"member": sibling},
            device_id_type=MESH,
        )

    def own_prior(half):
        return pltpu.make_async_copy(window(chip, half), yrows(me, half), loc_sem.at[6 + half])

    def prior_sends(half):
        made = []
        for j in range(1, chips):
            c = lax.rem(chip + j, chips)
            made.append(prior_copy(c, me, c * CORES + core, half, j))
        made.append(prior_copy(chip, me, sibling, half, 0))
        return made

    def forward(half):
        for j in range(1, chips):
            c = lax.rem(chip + j, chips)
            source = c * CORES + core
            forward_copy(source, half, j).wait_recv()
            forward_copy(source, half, j).start()

    def gathered(half):
        own_prior(half).wait()
        for j in range(chips):
            c = lax.rem(chip + j, chips)
            forward_copy(c * CORES + (CORES - 1 - core), half, j).wait_recv()

    def other(j):
        return lax.rem(chip + j, chips) * CORES + (CORES - 1 - core), CORES * j + 1

    def start_state(t):
        for j in range(1, chips):
            for p, far in (across(j), other(j)):
                state_copy(p, far, t, me).start()

    for copy in own_copies:
        copy.wait()
    for copy in prior_sends(0):
        copy.start()
    own_prior(0).start()
    for t in range(per_dev):
        state_copy(sibling, 0, t, me).start()

    @pl.when(reg < regions - 1)
    def _():
        for copy in halo(0):
            copy.wait_recv()

    @pl.when(reg > 0)
    def _():
        for copy in halo(1):
            copy.wait_recv()

    for copy in prior_sends(1):
        copy.start()
    own_prior(1).start()

    pos0 = chip * (CORES * per_dev * OBS_TILE)
    nrow = width_chip // 128
    hpad = (nrow + 15) // 16 * 16
    slots = tobs.shape[1]
    first = me * per_dev
    lane = lax.broadcasted_iota(jnp.int32, (1, slots), 1)
    hi_iota = lax.broadcasted_iota(jnp.int32, (hpad, slots), 0)
    lo_iota = lax.broadcasted_iota(jnp.int32, (128, slots), 0)
    base = chip * (CORES * per_dev * OBS_TILE // 128)
    values[...] = jnp.concatenate([vw[pl.ds(base + h, 1), :] for h in range(nrow)], axis=1)
    rinv_row = jnp.concatenate([rw[pl.ds(base + h, 1), :] for h in range(nrow)], axis=1)
    place = lax.broadcasted_iota(jnp.int32, (1, width_chip), 1)
    centre0 = RIM + OBS_TILE // 2 + core * (per_dev * OBS_TILE)
    for t in range(per_dev):
        rel = tv[pl.ds(first + t, 1), :] - pos0
        live = lane < ts[first + t]
        hi = jnp.where(live, rel // 128, -1)
        lo = lax.rem(rel, 128)
        one_hi = jnp.where(hi_iota == hi, 1.0, 0.0).astype(BF16)
        one_lo = jnp.where(lo_iota == lo, 1.0, 0.0).astype(BF16)
        grid = mm_nt(one_hi, one_lo)
        mask = jnp.concatenate([grid[h : h + 1, :] for h in range(nrow)], axis=1)
        dist = jnp.abs(place - (centre0 + t * OBS_TILE)).astype(F32) / LOC
        roots[t] = jnp.sqrt(mask * rinv_row / (1.0 + dist * dist))

    chunk = 256
    tiles = range(per_dev)

    def perturb(half):
        for k in range(half_width // chunk):
            at = pl.ds(pl.multiple_of(begin(chip, half) + k * chunk, 128), chunk)
            y = yall[:, at].astype(F32)
            ybar = jnp.sum(y, axis=0, keepdims=True) * (1.0 / members)
            pert = y - ybar
            dep = values[:, at] - ybar
            for t in tiles:
                root = roots[t, :, at]
                high, low = split(pert * root)
                uh[t, :members, at] = high
                ul[t, :, at] = low
                scaled = jnp.broadcast_to(root * dep, (8, chunk))
                rough = scaled.astype(BF16).astype(F32)
                uh[t, members:, at] = jnp.concatenate([rough, scaled - rough], axis=0).astype(BF16)

    def products(t, half):
        at = pl.ds(pl.multiple_of(begin(chip, half), 128), half_width)
        both = uh[t, :, at]
        return mm_nt(both, both[:members]), mm_nt(both, ul[t, :, at])

    forward(0)
    gathered(0)
    perturb(0)
    for half in range(2):
        for copy in prior_sends(half):
            copy.wait_send()
    start_state(0)
    early = [products(t, 0) for t in tiles]
    forward(1)
    for t in range(1, per_dev):
        start_state(t)
    gathered(1)
    perturb(1)

    row_i = lax.broadcasted_iota(jnp.int32, (members, members), 0)
    col_i = lax.broadcasted_iota(jnp.int32, (members, members), 1)
    eye = jnp.where(row_i == col_i, 1.0, 0.0).astype(F32)
    cs = factors(members)

    def transform(t):
        late = products(t, 1)
        main, cross = early[t][0] + late[0], early[t][1] + late[1]
        half = cross[:members]
        amat = (members - 1.0) * eye + main[:members] + (half + half.T)
        mmat = amat * (1.0 / (members - 1.0))
        scale = jnp.sqrt(jnp.sum(jnp.sum(mmat * mmat, axis=0, keepdims=True), axis=1, keepdims=True))
        rhs = main[members : members + 1] + main[members + 8 : members + 9] + cross[members : members + 1]
        p = mmat / scale
        v = jnp.broadcast_to(rhs * (float(np.prod(cs)) / (members - 1.0)) / scale, (16, members))
        e = eye - cs[0] * p
        z = 1.5 * eye - 0.5 * p
        for level in range(max(len(cs), 2 * ITERS - 1)):
            if level < len(cs):
                e2, v2 = split(e), split(v)
            if level < len(cs) - 1:
                both = dot3(tuple(jnp.concatenate(x, axis=0) for x in zip(e2, v2)), e2)
                v = v + both[members:]
                e = (1.0 - cs[level + 1]) * eye + cs[level + 1] * both[:members]
            elif level == len(cs) - 1:
                v = v + dot3(v2, e2)
            if level < 2 * ITERS - 2:
                if level % 2 == 0:
                    p2 = split(p)
                    square = dot3(p2, p2)
                else:
                    p = 2.25 * p + dot3(split(square), split(0.25 * p - 1.5 * eye))
            if level >= 2 and level % 2 == 0 and level <= 2 * ITERS - 2:
                z = dot3(split(z), split(1.5 * eye - 0.5 * p))
        wt[t] = (z / jnp.sqrt(scale) + v[:1]).astype(BF16)

    def result_copy(p, j, n, source):
        return pltpu.make_async_remote_copy(
            src_ref=res.at[pl.ds(pl.multiple_of(p * rows, rows), rows), pl.ds(n * PIECE, PIECE)],
            dst_ref=out.at[:, pl.ds(pl.multiple_of(me * block + n * PIECE, 128), PIECE)],
            send_sem=os_sem.at[j, n],
            recv_sem=or_sem.at[source, n],
            device_id={"member": p},
            device_id_type=MESH,
        )

    def own_result(n):
        return pltpu.make_async_copy(
            res.at[pl.ds(pl.multiple_of(me * rows, rows), rows), pl.ds(n * PIECE, PIECE)],
            out.at[:, pl.ds(pl.multiple_of(me * block + n * PIECE, 128), PIECE)],
            own_sem.at[n],
        )

    pieces = block // PIECE
    for n in range(pieces):
        t = n * PIECE // cells
        if n * PIECE % cells == 0:
            transform(t)
            if t == 0:
                own_state.wait()
            for j in range(1, groups):
                p = peer(j)
                state_copy(p, j, t, p).wait_recv()
        for k in range(PIECE // chunk):
            at = slice(n * PIECE + k * chunk, n * PIECE + (k + 1) * chunk)
            x = xall[:, at].astype(F32)
            xbar = jnp.sum(x, axis=0, keepdims=True) * (1.0 / members)
            pert = (x - xbar).astype(BF16)
            res[:, at] = (xbar + mm(wt[t], pert)).astype(BF16)
        for j in range(1, groups):
            result_copy(peer(j), j, n, me).start()
        own_result(n).start()

    for n in range(pieces):
        own_result(n).wait()
        for j in range(1, groups):
            p = peer(j)
            result_copy(p, j, n, p).wait_recv()
        for j in range(1, groups):
            result_copy(peer(j), j, n, me).wait_send()
    for t in range(per_dev):
        state_copy(sibling, 0, t, me).wait_send()
        for j in range(1, chips):
            for p, far in (across(j), other(j)):
                state_copy(p, far, t, me).wait_send()
    for half in range(2):
        for j in range(1, chips):
            c = lax.rem(chip + j, chips)
            forward_copy(c * CORES + core, half, j).wait_send()

    @pl.when(reg > 0)
    def _():
        for copy in halo(0):
            copy.wait_send()

    @pl.when(reg < regions - 1)
    def _():
        for copy in halo(1):
            copy.wait_send()


def body(groups, regions, state_prior, obs_prior, obs_value, obs_rinv, tile_obs, tile_count):
    rows = state_prior.shape[0]
    tiles = tile_obs.shape[0]
    per_dev = tiles // groups
    cells = state_prior.shape[1] // tiles
    obs = obs_prior.shape[1]
    members = groups * rows
    chips = groups // CORES
    width_chip = obs + 2 * RIM - (chips - 1) * CORES * per_dev * OBS_TILE
    pieces = per_dev * cells // PIECE
    sizes = (groups, regions, rows, per_dev, cells, obs)
    dma = pltpu.SemaphoreType.DMA
    return pl.pallas_call(
        functools.partial(kernel, sizes),
        out_shape=pltpu.VMEM(state_prior.shape, state_prior.dtype),
        in_specs=[pl.BlockSpec(memory_space=pl.ANY)] * 6,
        out_specs=pl.BlockSpec(memory_space=pltpu.VMEM),
        scratch_shapes=[
            pltpu.VMEM((rows, obs + 2 * RIM), BF16),
            pltpu.VMEM(((obs + 2 * RIM) // 128, 128), F32),
            pltpu.VMEM(((obs + 2 * RIM) // 128, 128), F32),
            pltpu.VMEM(tile_obs.shape, jnp.int32),
            pltpu.SMEM(tile_count.shape, jnp.int32),
            pltpu.VMEM((per_dev, 1, width_chip), F32),
            pltpu.VMEM((1, width_chip), F32),
            pltpu.VMEM((members, width_chip), BF16),
            pltpu.VMEM((members, per_dev * cells), BF16),
            pltpu.VMEM((members, per_dev * cells), BF16),
            pltpu.VMEM((per_dev, members + 16, width_chip), BF16),
            pltpu.VMEM((per_dev, members, width_chip), BF16),
            pltpu.VMEM((per_dev, members, members), BF16),
            dma((8,)),
            dma((pieces,)),
            dma((6,)),
            dma((6,)),
            dma((chips, 2)),
            dma((groups, 2)),
            dma((chips, 2)),
            dma((groups, per_dev)),
            dma((groups, per_dev)),
            dma((groups, pieces)),
            dma((groups, pieces)),
        ],
        compiler_params=pltpu.CompilerParams(
            collective_id=0, has_side_effects=True, vmem_limit_bytes=57 * 1024 * 1024
        ),
        cost_estimate=pl.CostEstimate(flops=4_000_000_000, bytes_accessed=8_000_000, transcendentals=0),
    )(
        state_prior,
        obs_prior,
        obs_value.reshape(-1, 128),
        obs_rinv.reshape(-1, 128),
        tile_obs,
        tile_count,
    )


def solution(mesh):
    placed = (
        P("member", "region"),
        P("member", "region"),
        P("region"),
        P("region"),
        P("region", None),
        P("region"),
    )
    return jax.shard_map(
        functools.partial(body, mesh.shape["member"], mesh.shape["region"]),
        mesh=mesh,
        in_specs=placed,
        out_specs=P("member", "region"),
        check_vma=False,
    )
```

```python
import functools

import jax
import jax.numpy as jnp
import numpy as np
from jax import lax
from jax.experimental import pallas as pl
from jax.experimental.pallas import tpu as pltpu
from jax.sharding import PartitionSpec as P

OBS_TILE = 128
ITERS = 4
RIM = 1024
LOC = 512
CORES = 2
VALUE_MAX = 6.0
RINV_MAX = 0.3
SLOTS_HALF = 1024
PIECE = 512
MESH = pl.DeviceIdType.MESH
F32 = jnp.float32
BF16 = jnp.bfloat16


def split(a):
    high = a.astype(BF16)
    return high, (a - high.astype(F32)).astype(BF16)


def mm(a, b):
    return jnp.dot(a, b, preferred_element_type=F32)


def mm_nt(a, b):
    return lax.dot_general(a, b, (((1,), (1,)), ((), ())), preferred_element_type=F32)


def dot3(a, b):
    (ah, al), (bh, bl) = a, b
    return mm(jnp.concatenate([ah, ah, al], axis=1), jnp.concatenate([bh, bl, bh], axis=0))


def factors(members):
    apart = np.arange(-SLOTS_HALF, SLOTS_HALF) / LOC
    trace = RINV_MAX * np.sum(1.0 / (1.0 + apart * apart)) * members * VALUE_MAX**2
    low = 0.9 * (members - 1.0) / ((members - 1.0) * np.sqrt(members) + trace)
    scales = []
    while True:
        scales.append(float(2.0 / (1.0 + low)))
        rest = ((1.0 - low) / (1.0 + low)) ** 2
        if rest < 1e-7:
            return scales
        low = 1.0 - rest


def kernel(
    sizes,
    state, prior, value, rinv, tobs, tcount,
    out,
    pw, vw, rw, tv, ts, roots, values, yall, xall, res, uh, ul, wt,
    loc_sem, own_sem, hs_sem, hr_sem, ys_sem, yr_sem, fs_sem, ss_sem, sr_sem, os_sem, or_sem,
):
    groups, regions, rows, per_dev, cells, obs = sizes
    chips = groups // CORES
    members = groups * rows
    me = lax.axis_index("member")
    reg = lax.axis_index("region")
    chip, core = me // CORES, lax.rem(me, CORES)
    sibling = chip * CORES + (CORES - 1 - core)
    wide = obs + 2 * RIM
    width_chip = wide - (chips - 1) * CORES * per_dev * OBS_TILE
    half_width = width_chip // 2
    rim_rows = RIM // 128
    obs_rows = obs // 128
    block = per_dev * cells

    def peer(j):
        return lax.rem(me + j, groups)

    barrier = pltpu.get_barrier_semaphore()
    for j in range(1, groups):
        pl.semaphore_signal(barrier, inc=1, device_id={"member": peer(j)}, device_id_type=MESH)

    @pl.when(reg > 0)
    def _():
        pl.semaphore_signal(barrier, inc=1, device_id={"region": reg - 1}, device_id_type=MESH)

    @pl.when(reg < regions - 1)
    def _():
        pl.semaphore_signal(barrier, inc=1, device_id={"region": reg + 1}, device_id_type=MESH)

    own_copies = [
        pltpu.make_async_copy(prior, pw.at[:, pl.ds(RIM, obs)], loc_sem.at[0]),
        pltpu.make_async_copy(value, vw.at[pl.ds(rim_rows, obs_rows), :], loc_sem.at[1]),
        pltpu.make_async_copy(rinv, rw.at[pl.ds(rim_rows, obs_rows), :], loc_sem.at[2]),
        pltpu.make_async_copy(tobs, tv, loc_sem.at[4]),
        pltpu.make_async_copy(tcount, ts, loc_sem.at[5]),
    ]
    for copy in own_copies:
        copy.start()

    def state_copy(p, j, t, source):
        return pltpu.make_async_remote_copy(
            src_ref=state.at[:, pl.ds(pl.multiple_of(p * block + t * cells, 128), cells)],
            dst_ref=xall.at[pl.ds(pl.multiple_of(me * rows, rows), rows), pl.ds(t * cells, cells)],
            send_sem=ss_sem.at[j, t],
            recv_sem=sr_sem.at[source, t],
            device_id={"member": p},
            device_id_type=MESH,
        )

    def partner(j):
        flips = []
        for bit in range(max(chips - 1, 1).bit_length()):
            size = 2**bit
            flips.append(size * (1 - 2 * lax.rem(chip // size, 2)))
        if j in (1, 2) and chips > 2:
            one, two = (flips[0], flips[1]) if j == 1 else (flips[1], flips[0])
            return chip + one * (1 - core) + two * core
        return chip + sum(flips[bit] for bit in range(len(flips)) if j >> bit & 1)

    def across(j):
        return partner(j) * CORES + core, CORES * j

    own_state = pltpu.make_async_copy(
        state.at[:, pl.ds(pl.multiple_of(me * block, 128), block)],
        xall.at[pl.ds(pl.multiple_of(me * rows, rows), rows), :],
        loc_sem.at[3],
    )
    own_state.start()

    @pl.when(reg == 0)
    def _():
        pw[:, :RIM] = jnp.zeros((rows, RIM), BF16)
        vw[:rim_rows, :] = jnp.zeros((rim_rows, 128), F32)
        rw[:rim_rows, :] = jnp.zeros((rim_rows, 128), F32)

    @pl.when(reg == regions - 1)
    def _():
        pw[:, RIM + obs :] = jnp.zeros((rows, RIM), BF16)
        vw[rim_rows + obs_rows :, :] = jnp.zeros((rim_rows, 128), F32)
        rw[rim_rows + obs_rows :, :] = jnp.zeros((rim_rows, 128), F32)

    expected = groups - 1 + (reg > 0).astype(jnp.int32) + (reg < regions - 1).astype(jnp.int32)
    pl.semaphore_wait(barrier, expected)

    def halo(side):
        at = reg - 1 if side == 0 else reg + 1
        src, dst = (0, RIM + obs) if side == 0 else (obs - RIM, 0)
        src_row, dst_row = src // 128, dst // 128
        made = []
        for n, (a, b) in enumerate(
            (
                (prior.at[:, pl.ds(src, RIM)], pw.at[:, pl.ds(dst, RIM)]),
                (value.at[pl.ds(src_row, rim_rows), :], vw.at[pl.ds(dst_row, rim_rows), :]),
                (rinv.at[pl.ds(src_row, rim_rows), :], rw.at[pl.ds(dst_row, rim_rows), :]),
            )
        ):
            made.append(
                pltpu.make_async_remote_copy(
                    src_ref=a,
                    dst_ref=b,
                    send_sem=hs_sem.at[3 * side + n],
                    recv_sem=hr_sem.at[3 * side + n],
                    device_id={"region": at},
                    device_id_type=MESH,
                )
            )
        return made

    @pl.when(reg > 0)
    def _():
        for copy in halo(0):
            copy.start()

    @pl.when(reg < regions - 1)
    def _():
        for copy in halo(1):
            copy.start()

    def begin(c, half):
        inner = 1 - (2 * c) // chips
        return (inner if half == 0 else 1 - inner) * half_width

    def window(c, half):
        at = c * (CORES * per_dev * OBS_TILE) + begin(c, half)
        return pw.at[:, pl.ds(pl.multiple_of(at, 128), half_width)]

    def yrows(m, half):
        at = pl.multiple_of(begin(chip, half), 128)
        return yall.at[pl.ds(pl.multiple_of(m * rows, rows), rows), pl.ds(at, half_width)]

    def prior_copy(c, source, to, half, j):
        at = pl.multiple_of(begin(c, half), 128)
        return pltpu.make_async_remote_copy(
            src_ref=window(c, half),
            dst_ref=yall.at[pl.ds(pl.multiple_of(source * rows, rows), rows), pl.ds(at, half_width)],
            send_sem=ys_sem.at[j, half],
            recv_sem=yr_sem.at[source, half],
            device_id={"member": to},
            device_id_type=MESH,
        )

    def forward_copy(source, half, j):
        return pltpu.make_async_remote_copy(
            src_ref=yrows(source, half),
            dst_ref=yrows(source, half),
            send_sem=fs_sem.at[j, half],
            recv_sem=yr_sem.at[source, half],
            device_id={"member": sibling},
            device_id_type=MESH,
        )

    def own_prior(half):
        return pltpu.make_async_copy(window(chip, half), yrows(me, half), loc_sem.at[6 + half])

    def prior_sends(half):
        made = []
        for j in range(1, chips):
            c = partner(j)
            made.append(prior_copy(c, me, c * CORES + core, half, j))
        made.append(prior_copy(chip, me, sibling, half, 0))
        return made

    def forward(half):
        for j in range(1, chips):
            c = lax.rem(chip + j, chips)
            source = c * CORES + core
            forward_copy(source, half, j).wait_recv()
            forward_copy(source, half, j).start()

    def gathered(half):
        own_prior(half).wait()
        for j in range(chips):
            c = lax.rem(chip + j, chips)
            forward_copy(c * CORES + (CORES - 1 - core), half, j).wait_recv()

    def other(j):
        return partner(j) * CORES + (CORES - 1 - core), CORES * j + 1

    def others():
        return [make(j) for j in range(1, chips) for make in (across, other)]

    early_state = [across(j) for j in range(1, min(chips, 3))]

    def start_state(t):
        for p, far in others():
            if t > 0 or far not in [place for _, place in early_state]:
                state_copy(p, far, t, me).start()

    for copy in own_copies:
        copy.wait()
    for copy in prior_sends(0):
        copy.start()
    own_prior(0).start()
    for t in range(per_dev):
        state_copy(sibling, 0, t, me).start()

    @pl.when(reg < regions - 1)
    def _():
        for copy in halo(0):
            copy.wait_recv()

    @pl.when(reg > 0)
    def _():
        for copy in halo(1):
            copy.wait_recv()

    for copy in prior_sends(1):
        copy.start()
    own_prior(1).start()
    for p, far in early_state:
        state_copy(p, far, 0, me).start()

    pos0 = chip * (CORES * per_dev * OBS_TILE)
    nrow = width_chip // 128
    hpad = (nrow + 15) // 16 * 16
    slots = tobs.shape[1]
    first = me * per_dev
    lane = lax.broadcasted_iota(jnp.int32, (1, slots), 1)
    hi_iota = lax.broadcasted_iota(jnp.int32, (hpad, slots), 0)
    lo_iota = lax.broadcasted_iota(jnp.int32, (128, slots), 0)
    base = chip * (CORES * per_dev * OBS_TILE // 128)
    values[...] = jnp.concatenate([vw[pl.ds(base + h, 1), :] for h in range(nrow)], axis=1)
    rinv_row = jnp.concatenate([rw[pl.ds(base + h, 1), :] for h in range(nrow)], axis=1)
    place = lax.broadcasted_iota(jnp.int32, (1, width_chip), 1)
    centre0 = RIM + OBS_TILE // 2 + core * (per_dev * OBS_TILE)
    for t in range(per_dev):
        rel = tv[pl.ds(first + t, 1), :] - pos0
        live = lane < ts[first + t]
        hi = jnp.where(live, rel // 128, -1)
        lo = lax.rem(rel, 128)
        one_hi = jnp.where(hi_iota == hi, 1.0, 0.0).astype(BF16)
        one_lo = jnp.where(lo_iota == lo, 1.0, 0.0).astype(BF16)
        grid = mm_nt(one_hi, one_lo)
        mask = jnp.concatenate([grid[h : h + 1, :] for h in range(nrow)], axis=1)
        dist = jnp.abs(place - (centre0 + t * OBS_TILE)).astype(F32) / LOC
        roots[t] = jnp.sqrt(mask * rinv_row / (1.0 + dist * dist))

    chunk = 256
    tiles = range(per_dev)

    def perturb(half):
        for k in range(half_width // chunk):
            at = pl.ds(pl.multiple_of(begin(chip, half) + k * chunk, 128), chunk)
            y = yall[:, at].astype(F32)
            ybar = jnp.sum(y, axis=0, keepdims=True) * (1.0 / members)
            pert = y - ybar
            dep = values[:, at] - ybar
            for t in tiles:
                root = roots[t, :, at]
                high, low = split(pert * root)
                uh[t, :members, at] = high
                ul[t, :, at] = low
                scaled = jnp.broadcast_to(root * dep, (8, chunk))
                rough = scaled.astype(BF16).astype(F32)
                uh[t, members:, at] = jnp.concatenate([rough, scaled - rough], axis=0).astype(BF16)

    def products(t, half):
        at = pl.ds(pl.multiple_of(begin(chip, half), 128), half_width)
        both = uh[t, :, at]
        return mm_nt(both, both[:members]), mm_nt(both, ul[t, :, at])

    forward(0)
    gathered(0)
    perturb(0)
    forward(1)
    for t in tiles:
        start_state(t)
    early = [products(t, 0) for t in tiles]
    for half in range(2):
        for copy in prior_sends(half):
            copy.wait_send()
    gathered(1)
    perturb(1)

    row_i = lax.broadcasted_iota(jnp.int32, (members, members), 0)
    col_i = lax.broadcasted_iota(jnp.int32, (members, members), 1)
    eye = jnp.where(row_i == col_i, 1.0, 0.0).astype(F32)
    cs = factors(members)

    def transform(t):
        late = products(t, 1)
        main, cross = early[t][0] + late[0], early[t][1] + late[1]
        half = cross[:members]
        amat = (members - 1.0) * eye + main[:members] + (half + half.T)
        mmat = amat * (1.0 / (members - 1.0))
        scale = jnp.sqrt(jnp.sum(jnp.sum(mmat * mmat, axis=0, keepdims=True), axis=1, keepdims=True))
        rhs = main[members : members + 1] + main[members + 8 : members + 9] + cross[members : members + 1]
        p = mmat / scale
        v = jnp.broadcast_to(rhs * (float(np.prod(cs)) / (members - 1.0)) / scale, (16, members))
        e = eye - cs[0] * p
        z = 1.5 * eye - 0.5 * p
        for level in range(max(len(cs), 2 * ITERS - 1)):
            if level < len(cs):
                e2, v2 = split(e), split(v)
            if level < len(cs) - 1:
                both = dot3(tuple(jnp.concatenate(x, axis=0) for x in zip(e2, v2)), e2)
                v = v + both[members:]
                e = (1.0 - cs[level + 1]) * eye + cs[level + 1] * both[:members]
            elif level == len(cs) - 1:
                v = v + dot3(v2, e2)
            if level < 2 * ITERS - 2:
                if level % 2 == 0:
                    p2 = split(p)
                    square = dot3(p2, p2)
                else:
                    p = 2.25 * p + dot3(split(square), split(0.25 * p - 1.5 * eye))
            if level >= 2 and level % 2 == 0 and level <= 2 * ITERS - 2:
                z = dot3(split(z), split(1.5 * eye - 0.5 * p))
        wt[t] = (z / jnp.sqrt(scale) + v[:1]).astype(BF16)

    def result_copy(p, j, n, source):
        return pltpu.make_async_remote_copy(
            src_ref=res.at[pl.ds(pl.multiple_of(p * rows, rows), rows), pl.ds(n * PIECE, PIECE)],
            dst_ref=out.at[:, pl.ds(pl.multiple_of(me * block + n * PIECE, 128), PIECE)],
            send_sem=os_sem.at[j, n],
            recv_sem=or_sem.at[source, n],
            device_id={"member": p},
            device_id_type=MESH,
        )

    def own_result(n):
        return pltpu.make_async_copy(
            res.at[pl.ds(pl.multiple_of(me * rows, rows), rows), pl.ds(n * PIECE, PIECE)],
            out.at[:, pl.ds(pl.multiple_of(me * block + n * PIECE, 128), PIECE)],
            own_sem.at[n],
        )

    pieces = block // PIECE
    for n in range(pieces):
        t = n * PIECE // cells
        if n * PIECE % cells == 0:
            transform(t)
            if t == 0:
                own_state.wait()
            for j in range(1, groups):
                p = peer(j)
                state_copy(p, j, t, p).wait_recv()
        for k in range(PIECE // chunk):
            at = slice(n * PIECE + k * chunk, n * PIECE + (k + 1) * chunk)
            x = xall[:, at].astype(F32)
            xbar = jnp.sum(x, axis=0, keepdims=True) * (1.0 / members)
            pert = (x - xbar).astype(BF16)
            res[:, at] = (xbar + mm(wt[t], pert)).astype(BF16)
        for p, far in [(sibling, 0)] + others():
            result_copy(p, far, n, me).start()
        own_result(n).start()

    for n in range(pieces):
        own_result(n).wait()
        for j in range(1, groups):
            p = peer(j)
            result_copy(p, j, n, p).wait_recv()
        for p, far in [(sibling, 0)] + others():
            result_copy(p, far, n, me).wait_send()
    for t in range(per_dev):
        state_copy(sibling, 0, t, me).wait_send()
        for p, far in others():
            state_copy(p, far, t, me).wait_send()
    for half in range(2):
        for j in range(1, chips):
            c = lax.rem(chip + j, chips)
            forward_copy(c * CORES + core, half, j).wait_send()

    @pl.when(reg > 0)
    def _():
        for copy in halo(0):
            copy.wait_send()

    @pl.when(reg < regions - 1)
    def _():
        for copy in halo(1):
            copy.wait_send()


def body(groups, regions, state_prior, obs_prior, obs_value, obs_rinv, tile_obs, tile_count):
    rows = state_prior.shape[0]
    tiles = tile_obs.shape[0]
    per_dev = tiles // groups
    cells = state_prior.shape[1] // tiles
    obs = obs_prior.shape[1]
    members = groups * rows
    chips = groups // CORES
    width_chip = obs + 2 * RIM - (chips - 1) * CORES * per_dev * OBS_TILE
    pieces = per_dev * cells // PIECE
    sizes = (groups, regions, rows, per_dev, cells, obs)
    dma = pltpu.SemaphoreType.DMA
    return pl.pallas_call(
        functools.partial(kernel, sizes),
        out_shape=pltpu.VMEM(state_prior.shape, state_prior.dtype),
        in_specs=[pl.BlockSpec(memory_space=pl.ANY)] * 6,
        out_specs=pl.BlockSpec(memory_space=pltpu.VMEM),
        scratch_shapes=[
            pltpu.VMEM((rows, obs + 2 * RIM), BF16),
            pltpu.VMEM(((obs + 2 * RIM) // 128, 128), F32),
            pltpu.VMEM(((obs + 2 * RIM) // 128, 128), F32),
            pltpu.VMEM(tile_obs.shape, jnp.int32),
            pltpu.SMEM(tile_count.shape, jnp.int32),
            pltpu.VMEM((per_dev, 1, width_chip), F32),
            pltpu.VMEM((1, width_chip), F32),
            pltpu.VMEM((members, width_chip), BF16),
            pltpu.VMEM((members, per_dev * cells), BF16),
            pltpu.VMEM((members, per_dev * cells), BF16),
            pltpu.VMEM((per_dev, members + 16, width_chip), BF16),
            pltpu.VMEM((per_dev, members, width_chip), BF16),
            pltpu.VMEM((per_dev, members, members), BF16),
            dma((8,)),
            dma((pieces,)),
            dma((6,)),
            dma((6,)),
            dma((chips, 2)),
            dma((groups, 2)),
            dma((chips, 2)),
            dma((groups, per_dev)),
            dma((groups, per_dev)),
            dma((groups, pieces)),
            dma((groups, pieces)),
        ],
        compiler_params=pltpu.CompilerParams(
            collective_id=0, has_side_effects=True, vmem_limit_bytes=57 * 1024 * 1024
        ),
        cost_estimate=pl.CostEstimate(flops=4_000_000_000, bytes_accessed=8_000_000, transcendentals=0),
    )(
        state_prior,
        obs_prior,
        obs_value.reshape(-1, 128),
        obs_rinv.reshape(-1, 128),
        tile_obs,
        tile_count,
    )


def solution(mesh):
    placed = (
        P("member", "region"),
        P("member", "region"),
        P("region"),
        P("region"),
        P("region", None),
        P("region"),
    )
    return jax.shard_map(
        functools.partial(body, mesh.shape["member"], mesh.shape["region"]),
        mesh=mesh,
        in_specs=placed,
        out_specs=P("member", "region"),
        check_vma=False,
    )
```

```python
import functools

import jax
import jax.numpy as jnp
import numpy as np
from jax import lax
from jax.experimental import pallas as pl
from jax.experimental.pallas import tpu as pltpu
from jax.sharding import PartitionSpec as P

OBS_TILE = 128
ITERS = 4
RIM = 1024
LOC = 512
CORES = 2
VALUE_MAX = 6.0
RINV_MAX = 0.3
SLOTS_HALF = 1024
PIECE = 512
MESH = pl.DeviceIdType.MESH
F32 = jnp.float32
BF16 = jnp.bfloat16


def split(a):
    high = a.astype(BF16)
    return high, (a - high.astype(F32)).astype(BF16)


def mm(a, b):
    return jnp.dot(a, b, preferred_element_type=F32)


def mm_nt(a, b):
    return lax.dot_general(a, b, (((1,), (1,)), ((), ())), preferred_element_type=F32)


def dot3(a, b):
    (ah, al), (bh, bl) = a, b
    return mm(jnp.concatenate([ah, ah, al], axis=1), jnp.concatenate([bh, bl, bh], axis=0))


def factors(members):
    apart = np.arange(-SLOTS_HALF, SLOTS_HALF) / LOC
    trace = RINV_MAX * np.sum(1.0 / (1.0 + apart * apart)) * members * VALUE_MAX**2
    low = 0.9 * (members - 1.0) / ((members - 1.0) * np.sqrt(members) + trace)
    scales = []
    while True:
        scales.append(float(2.0 / (1.0 + low)))
        rest = ((1.0 - low) / (1.0 + low)) ** 2
        if rest < 1e-7:
            return scales
        low = 1.0 - rest


def kernel(
    sizes,
    state, prior, value, rinv, tobs, tcount,
    out,
    vw, rw, tv, ts, roots, values, yall, xall, res, uh, ul, wt,
    loc_sem, own_sem, hs_sem, hr_sem, ys_sem, yr_sem, fs_sem, zs_sem, ss_sem, sr_sem, os_sem, or_sem,
):
    groups, regions, rows, per_dev, cells, obs = sizes
    chips = groups // CORES
    members = groups * rows
    me = lax.axis_index("member")
    reg = lax.axis_index("region")
    chip, core = me // CORES, lax.rem(me, CORES)
    sibling = chip * CORES + (CORES - 1 - core)
    wide = obs + 2 * RIM
    width_chip = wide - (chips - 1) * CORES * per_dev * OBS_TILE
    half_width = width_chip // 2
    rim_rows = RIM // 128
    obs_rows = obs // 128
    block = per_dev * cells

    def peer(j):
        return lax.rem(me + j, groups)

    barrier = pltpu.get_barrier_semaphore()
    for j in range(1, groups):
        pl.semaphore_signal(barrier, inc=1, device_id={"member": peer(j)}, device_id_type=MESH)

    @pl.when(reg > 0)
    def _():
        pl.semaphore_signal(barrier, inc=1, device_id={"region": reg - 1}, device_id_type=MESH)

    @pl.when(reg < regions - 1)
    def _():
        pl.semaphore_signal(barrier, inc=1, device_id={"region": reg + 1}, device_id_type=MESH)

    own_copies = [
        pltpu.make_async_copy(
            prior, yall.at[pl.ds(pl.multiple_of(me * rows, rows), rows), pl.ds(RIM, obs)], loc_sem.at[0]
        ),
        pltpu.make_async_copy(value, vw.at[pl.ds(rim_rows, obs_rows), :], loc_sem.at[1]),
        pltpu.make_async_copy(rinv, rw.at[pl.ds(rim_rows, obs_rows), :], loc_sem.at[2]),
        pltpu.make_async_copy(tobs, tv, loc_sem.at[4]),
        pltpu.make_async_copy(tcount, ts, loc_sem.at[5]),
    ]
    for copy in own_copies:
        copy.start()

    def state_copy(p, j, t, source):
        return pltpu.make_async_remote_copy(
            src_ref=state.at[:, pl.ds(pl.multiple_of(p * block + t * cells, 128), cells)],
            dst_ref=xall.at[pl.ds(pl.multiple_of(me * rows, rows), rows), pl.ds(t * cells, cells)],
            send_sem=ss_sem.at[j, t],
            recv_sem=sr_sem.at[source, t],
            device_id={"member": p},
            device_id_type=MESH,
        )

    def partner(j):
        flips = []
        for bit in range(max(chips - 1, 1).bit_length()):
            size = 2**bit
            flips.append(size * (1 - 2 * lax.rem(chip // size, 2)))
        if j in (1, 2) and chips > 2:
            one, two = (flips[0], flips[1]) if j == 1 else (flips[1], flips[0])
            return chip + one * (1 - core) + two * core
        return chip + sum(flips[bit] for bit in range(len(flips)) if j >> bit & 1)

    def across(j):
        return partner(j) * CORES + core, CORES * j

    own_state = pltpu.make_async_copy(
        state.at[:, pl.ds(pl.multiple_of(me * block, 128), block)],
        xall.at[pl.ds(pl.multiple_of(me * rows, rows), rows), :],
        loc_sem.at[3],
    )
    own_state.start()

    @pl.when(reg == 0)
    def _():
        yall[:, :RIM] = jnp.zeros((members, RIM), BF16)
        vw[:rim_rows, :] = jnp.zeros((rim_rows, 128), F32)
        rw[:rim_rows, :] = jnp.zeros((rim_rows, 128), F32)

    @pl.when(reg == regions - 1)
    def _():
        yall[:, RIM + obs :] = jnp.zeros((members, RIM), BF16)
        vw[rim_rows + obs_rows :, :] = jnp.zeros((rim_rows, 128), F32)
        rw[rim_rows + obs_rows :, :] = jnp.zeros((rim_rows, 128), F32)

    expected = groups - 1 + (reg > 0).astype(jnp.int32) + (reg < regions - 1).astype(jnp.int32)
    pl.semaphore_wait(barrier, expected)

    def halo(side):
        at = reg - 1 if side == 0 else reg + 1
        src, dst = (0, RIM + obs) if side == 0 else (obs - RIM, 0)
        src_row, dst_row = src // 128, dst // 128
        made = []
        for n, (a, b) in enumerate(
            (
                (value.at[pl.ds(src_row, rim_rows), :], vw.at[pl.ds(dst_row, rim_rows), :]),
                (rinv.at[pl.ds(src_row, rim_rows), :], rw.at[pl.ds(dst_row, rim_rows), :]),
            )
        ):
            made.append(
                pltpu.make_async_remote_copy(
                    src_ref=a,
                    dst_ref=b,
                    send_sem=hs_sem.at[2 * side + n],
                    recv_sem=hr_sem.at[2 * side + n],
                    device_id={"region": at},
                    device_id_type=MESH,
                )
            )
        return made

    @pl.when(reg > 0)
    def _():
        for copy in halo(0):
            copy.start()

    @pl.when(reg < regions - 1)
    def _():
        for copy in halo(1):
            copy.start()

    bits = (chips - 1).bit_length()
    orders = (list(range(bits)), list(range(bits))[::-1])
    upper = (2 * chip) // chips
    to_region = reg + 1 - 2 * upper
    from_region = reg - 1 + 2 * upper
    can_send = jnp.logical_and(to_region >= 0, to_region < regions)
    can_receive = jnp.logical_and(from_region >= 0, from_region < regions)

    def flipped(mask):
        return chip + sum(
            2**bit * (1 - 2 * lax.rem(chip // 2**bit, 2)) for bit in range(bits) if mask >> bit & 1
        )

    def member(mask):
        return flipped(mask) * CORES + core

    def yblock(m, part):
        if part < 2:
            columns = pl.ds(RIM + part * (obs // 2), obs // 2)
        else:
            columns = pl.ds(pl.multiple_of(upper * (RIM + obs), 128), RIM)
        return yall.at[pl.ds(pl.multiple_of(m * rows, rows), rows), columns]

    def prior_copy(m, part, send_sem, device):
        return pltpu.make_async_remote_copy(
            src_ref=yblock(m, part),
            dst_ref=yblock(m, part),
            send_sem=send_sem,
            recv_sem=yr_sem.at[m, part],
            device_id=device,
            device_id_type=MESH,
        )

    def stage_copies(half, stage):
        flip = 1 << orders[half][stage]
        made = []
        for mask in range(chips):
            if not any(mask >> bit & 1 for bit in orders[half][stage:]):
                made.append(prior_copy(member(mask), half, ys_sem.at[mask ^ flip, half], {"member": member(flip)}))
        return made

    def stage_masks(half, stage):
        flip = 1 << orders[half][stage]
        return [
            mask for mask in range(chips)
            if mask & flip and not any(mask >> bit & 1 for bit in orders[half][stage + 1 :])
        ]

    def forward_copy(mask, part):
        return prior_copy(member(mask), part, fs_sem.at[mask, part], {"member": sibling})

    def plane_copy(mask):
        source = pl.ds(pl.multiple_of(obs + upper * (RIM - obs), 128), RIM)
        m = member(mask)
        return pltpu.make_async_remote_copy(
            src_ref=yall.at[pl.ds(pl.multiple_of(m * rows, rows), rows), source],
            dst_ref=yblock(m, 2),
            send_sem=zs_sem.at[mask],
            recv_sem=yr_sem.at[m, 2],
            device_id={"region": to_region},
            device_id_type=MESH,
        )

    def arrived(half, mask):
        @pl.when(jnp.logical_and(can_send, upper == 1 - half))
        def _():
            plane_copy(mask).start()

        forward_copy(mask, half).start()

    def receive(half, stage):
        for mask in stage_masks(half, stage):
            forward_copy(mask, half).wait_recv()

    def gathered():
        for m in range(chips):
            for half in range(2):
                forward_copy_from(m, half).wait_recv()

    def forward_copy_from(c, part):
        return prior_copy(c * CORES + (CORES - 1 - core), part, fs_sem.at[0, part], {"member": sibling})

    def begin(c, half):
        inner = 1 - (2 * c) // chips
        return (inner if half == 0 else 1 - inner) * half_width

    def other(j):
        return partner(j) * CORES + (CORES - 1 - core), CORES * j + 1

    def others():
        return [make(j) for j in range(1, chips) for make in (across, other)]

    early_state = [across(j) for j in range(1, min(chips, 3))]

    def start_state(t):
        for p, far in others():
            if t > 0 or far not in [place for _, place in early_state]:
                state_copy(p, far, t, me).start()

    for copy in own_copies:
        copy.wait()
    for half in range(2):
        for copy in stage_copies(half, 0):
            copy.start()
    for half in range(2):
        arrived(half, 0)
    for t in range(per_dev):
        state_copy(sibling, 0, t, me).start()
    for stage in range(1, bits):
        for half in range(2):
            receive(half, stage - 1)
            for copy in stage_copies(half, stage):
                copy.start()
            for mask in stage_masks(half, stage - 1):
                arrived(half, mask)
    for p, far in early_state:
        state_copy(p, far, 0, me).start()

    @pl.when(reg < regions - 1)
    def _():
        for copy in halo(0):
            copy.wait_recv()

    @pl.when(reg > 0)
    def _():
        for copy in halo(1):
            copy.wait_recv()

    pos0 = chip * (CORES * per_dev * OBS_TILE)
    nrow = width_chip // 128
    hpad = (nrow + 15) // 16 * 16
    slots = tobs.shape[1]
    first = me * per_dev
    lane = lax.broadcasted_iota(jnp.int32, (1, slots), 1)
    hi_iota = lax.broadcasted_iota(jnp.int32, (hpad, slots), 0)
    lo_iota = lax.broadcasted_iota(jnp.int32, (128, slots), 0)
    base = chip * (CORES * per_dev * OBS_TILE // 128)
    values[...] = jnp.concatenate([vw[pl.ds(base + h, 1), :] for h in range(nrow)], axis=1)
    rinv_row = jnp.concatenate([rw[pl.ds(base + h, 1), :] for h in range(nrow)], axis=1)
    place = lax.broadcasted_iota(jnp.int32, (1, width_chip), 1)
    centre0 = RIM + OBS_TILE // 2 + core * (per_dev * OBS_TILE)
    for t in range(per_dev):
        rel = tv[pl.ds(first + t, 1), :] - pos0
        live = lane < ts[first + t]
        hi = jnp.where(live, rel // 128, -1)
        lo = lax.rem(rel, 128)
        one_hi = jnp.where(hi_iota == hi, 1.0, 0.0).astype(BF16)
        one_lo = jnp.where(lo_iota == lo, 1.0, 0.0).astype(BF16)
        grid = mm_nt(one_hi, one_lo)
        mask = jnp.concatenate([grid[h : h + 1, :] for h in range(nrow)], axis=1)
        dist = jnp.abs(place - (centre0 + t * OBS_TILE)).astype(F32) / LOC
        roots[t] = jnp.sqrt(mask * rinv_row / (1.0 + dist * dist))

    chunk = 256
    tiles = range(per_dev)

    def perturb(half):
        for k in range(half_width // chunk):
            at = pl.ds(pl.multiple_of(begin(chip, half) + k * chunk, 128), chunk)
            y = yall[:, pl.ds(pl.multiple_of(pos0 + begin(chip, half) + k * chunk, 128), chunk)].astype(F32)
            ybar = jnp.sum(y, axis=0, keepdims=True) * (1.0 / members)
            pert = y - ybar
            dep = values[:, at] - ybar
            for t in tiles:
                root = roots[t, :, at]
                high, low = split(pert * root)
                uh[t, :members, at] = high
                ul[t, :, at] = low
                scaled = jnp.broadcast_to(root * dep, (8, chunk))
                rough = scaled.astype(BF16).astype(F32)
                uh[t, members:, at] = jnp.concatenate([rough, scaled - rough], axis=0).astype(BF16)

    def products(t, half):
        at = pl.ds(pl.multiple_of(begin(chip, half), 128), half_width)
        both = uh[t, :, at]
        return mm_nt(both, both[:members]), mm_nt(both, ul[t, :, at])

    for half in range(2):
        receive(half, bits - 1)
        for mask in stage_masks(half, bits - 1):
            arrived(half, mask)
    start_state(0)
    gathered()
    perturb(0)

    @pl.when(can_receive)
    def _():
        for mask in range(chips):
            forward_copy(mask, 2).wait_recv()
            forward_copy(mask, 2).start()

    for t in range(1, per_dev):
        start_state(t)
    early = [products(t, 0) for t in tiles]

    @pl.when(can_receive)
    def _():
        for c in range(chips):
            forward_copy_from(c, 2).wait_recv()

    perturb(1)

    row_i = lax.broadcasted_iota(jnp.int32, (members, members), 0)
    col_i = lax.broadcasted_iota(jnp.int32, (members, members), 1)
    eye = jnp.where(row_i == col_i, 1.0, 0.0).astype(F32)
    cs = factors(members)

    def transform(t):
        late = products(t, 1)
        main, cross = early[t][0] + late[0], early[t][1] + late[1]
        half = cross[:members]
        amat = (members - 1.0) * eye + main[:members] + (half + half.T)
        mmat = amat * (1.0 / (members - 1.0))
        scale = jnp.sqrt(jnp.sum(jnp.sum(mmat * mmat, axis=0, keepdims=True), axis=1, keepdims=True))
        rhs = main[members : members + 1] + main[members + 8 : members + 9] + cross[members : members + 1]
        p = mmat / scale
        v = jnp.broadcast_to(rhs * (float(np.prod(cs)) / (members - 1.0)) / scale, (16, members))
        e = eye - cs[0] * p
        z = 1.5 * eye - 0.5 * p
        for level in range(max(len(cs), 2 * ITERS - 1)):
            if level < len(cs):
                e2, v2 = split(e), split(v)
            if level < len(cs) - 1:
                both = dot3(tuple(jnp.concatenate(x, axis=0) for x in zip(e2, v2)), e2)
                v = v + both[members:]
                e = (1.0 - cs[level + 1]) * eye + cs[level + 1] * both[:members]
            elif level == len(cs) - 1:
                v = v + dot3(v2, e2)
            if level < 2 * ITERS - 2:
                if level % 2 == 0:
                    p2 = split(p)
                    square = dot3(p2, p2)
                else:
                    p = 2.25 * p + dot3(split(square), split(0.25 * p - 1.5 * eye))
            if level >= 2 and level % 2 == 0 and level <= 2 * ITERS - 2:
                z = dot3(split(z), split(1.5 * eye - 0.5 * p))
        wt[t] = (z / jnp.sqrt(scale) + v[:1]).astype(BF16)

    def result_copy(p, j, n, source):
        return pltpu.make_async_remote_copy(
            src_ref=res.at[pl.ds(pl.multiple_of(p * rows, rows), rows), pl.ds(n * PIECE, PIECE)],
            dst_ref=out.at[:, pl.ds(pl.multiple_of(me * block + n * PIECE, 128), PIECE)],
            send_sem=os_sem.at[j, n],
            recv_sem=or_sem.at[source, n],
            device_id={"member": p},
            device_id_type=MESH,
        )

    def own_result(n):
        return pltpu.make_async_copy(
            res.at[pl.ds(pl.multiple_of(me * rows, rows), rows), pl.ds(n * PIECE, PIECE)],
            out.at[:, pl.ds(pl.multiple_of(me * block + n * PIECE, 128), PIECE)],
            own_sem.at[n],
        )

    pieces = block // PIECE
    for n in range(pieces):
        t = n * PIECE // cells
        if n * PIECE % cells == 0:
            transform(t)
            if t == 0:
                own_state.wait()
            for j in range(1, groups):
                p = peer(j)
                state_copy(p, j, t, p).wait_recv()
        for k in range(PIECE // chunk):
            at = slice(n * PIECE + k * chunk, n * PIECE + (k + 1) * chunk)
            x = xall[:, at].astype(F32)
            xbar = jnp.sum(x, axis=0, keepdims=True) * (1.0 / members)
            pert = (x - xbar).astype(BF16)
            res[:, at] = (xbar + mm(wt[t], pert)).astype(BF16)
        for p, far in [(sibling, 0)] + others():
            result_copy(p, far, n, me).start()
        own_result(n).start()

    for n in range(pieces):
        own_result(n).wait()
        for j in range(1, groups):
            p = peer(j)
            result_copy(p, j, n, p).wait_recv()
        for p, far in [(sibling, 0)] + others():
            result_copy(p, far, n, me).wait_send()
    for t in range(per_dev):
        state_copy(sibling, 0, t, me).wait_send()
        for p, far in others():
            state_copy(p, far, t, me).wait_send()
    for half in range(2):
        for stage in range(bits):
            for copy in stage_copies(half, stage):
                copy.wait_send()
        for mask in range(chips):
            forward_copy(mask, half).wait_send()

    @pl.when(can_send)
    def _():
        for mask in range(chips):
            plane_copy(mask).wait_send()

    @pl.when(can_receive)
    def _():
        for mask in range(chips):
            forward_copy(mask, 2).wait_send()

    @pl.when(reg > 0)
    def _():
        for copy in halo(0):
            copy.wait_send()

    @pl.when(reg < regions - 1)
    def _():
        for copy in halo(1):
            copy.wait_send()


def body(groups, regions, state_prior, obs_prior, obs_value, obs_rinv, tile_obs, tile_count):
    rows = state_prior.shape[0]
    tiles = tile_obs.shape[0]
    per_dev = tiles // groups
    cells = state_prior.shape[1] // tiles
    obs = obs_prior.shape[1]
    members = groups * rows
    chips = groups // CORES
    width_chip = obs + 2 * RIM - (chips - 1) * CORES * per_dev * OBS_TILE
    pieces = per_dev * cells // PIECE
    sizes = (groups, regions, rows, per_dev, cells, obs)
    dma = pltpu.SemaphoreType.DMA
    return pl.pallas_call(
        functools.partial(kernel, sizes),
        out_shape=pltpu.VMEM(state_prior.shape, state_prior.dtype),
        in_specs=[pl.BlockSpec(memory_space=pl.ANY)] * 6,
        out_specs=pl.BlockSpec(memory_space=pltpu.VMEM),
        scratch_shapes=[
            pltpu.VMEM(((obs + 2 * RIM) // 128, 128), F32),
            pltpu.VMEM(((obs + 2 * RIM) // 128, 128), F32),
            pltpu.VMEM(tile_obs.shape, jnp.int32),
            pltpu.SMEM(tile_count.shape, jnp.int32),
            pltpu.VMEM((per_dev, 1, width_chip), F32),
            pltpu.VMEM((1, width_chip), F32),
            pltpu.VMEM((members, obs + 2 * RIM), BF16),
            pltpu.VMEM((members, per_dev * cells), BF16),
            pltpu.VMEM((members, per_dev * cells), BF16),
            pltpu.VMEM((per_dev, members + 16, width_chip), BF16),
            pltpu.VMEM((per_dev, members, width_chip), BF16),
            pltpu.VMEM((per_dev, members, members), BF16),
            dma((8,)),
            dma((pieces,)),
            dma((4,)),
            dma((4,)),
            dma((chips, 2)),
            dma((groups, 3)),
            dma((chips, 3)),
            dma((chips,)),
            dma((groups, per_dev)),
            dma((groups, per_dev)),
            dma((groups, pieces)),
            dma((groups, pieces)),
        ],
        compiler_params=pltpu.CompilerParams(
            collective_id=0, has_side_effects=True, vmem_limit_bytes=57 * 1024 * 1024
        ),
        cost_estimate=pl.CostEstimate(flops=4_000_000_000, bytes_accessed=8_000_000, transcendentals=0),
    )(
        state_prior,
        obs_prior,
        obs_value.reshape(-1, 128),
        obs_rinv.reshape(-1, 128),
        tile_obs,
        tile_count,
    )


def solution(mesh):
    placed = (
        P("member", "region"),
        P("member", "region"),
        P("region"),
        P("region"),
        P("region", None),
        P("region"),
    )
    return jax.shard_map(
        functools.partial(body, mesh.shape["member"], mesh.shape["region"]),
        mesh=mesh,
        in_specs=placed,
        out_specs=P("member", "region"),
        check_vma=False,
    )
```

```python
import functools

import jax
import jax.numpy as jnp
import numpy as np
from jax import lax
from jax.experimental import pallas as pl
from jax.experimental.pallas import tpu as pltpu
from jax.sharding import PartitionSpec as P

OBS_TILE = 128
ITERS = 4
RIM = 1024
LOC = 512
CORES = 2
VALUE_MAX = 6.0
RINV_MAX = 0.3
SLOTS_HALF = 1024
PIECE = 512
MESH = pl.DeviceIdType.MESH
F32 = jnp.float32
BF16 = jnp.bfloat16


def split(a):
    high = a.astype(BF16)
    return high, (a - high.astype(F32)).astype(BF16)


def mm(a, b):
    return jnp.dot(a, b, preferred_element_type=F32)


def mm_nt(a, b):
    return lax.dot_general(a, b, (((1,), (1,)), ((), ())), preferred_element_type=F32)


def dot3(a, b):
    (ah, al), (bh, bl) = a, b
    return mm(jnp.concatenate([ah, ah, al], axis=1), jnp.concatenate([bh, bl, bh], axis=0))


def factors(members):
    apart = np.arange(-SLOTS_HALF, SLOTS_HALF) / LOC
    trace = RINV_MAX * np.sum(1.0 / (1.0 + apart * apart)) * members * VALUE_MAX**2
    low = 0.9 * (members - 1.0) / ((members - 1.0) * np.sqrt(members) + trace)
    scales = []
    while True:
        scales.append(float(2.0 / (1.0 + low)))
        rest = ((1.0 - low) / (1.0 + low)) ** 2
        if rest < 1e-7:
            return scales
        low = 1.0 - rest


def kernel(
    sizes,
    state, prior, value, rinv, tobs, tcount,
    out,
    vw, rw, tv, ts, roots, values, yall, xall, res, uh, ul, wt,
    loc_sem, own_sem, hs_sem, hr_sem, ys_sem, yr_sem, fs_sem, zs_sem, ss_sem, sr_sem, os_sem, or_sem,
):
    groups, regions, rows, per_dev, cells, obs = sizes
    chips = groups // CORES
    members = groups * rows
    me = lax.axis_index("member")
    reg = lax.axis_index("region")
    chip, core = me // CORES, lax.rem(me, CORES)
    sibling = chip * CORES + (CORES - 1 - core)
    wide = obs + 2 * RIM
    width_chip = wide - (chips - 1) * CORES * per_dev * OBS_TILE
    half_width = width_chip // 2
    rim_rows = RIM // 128
    obs_rows = obs // 128
    block = per_dev * cells

    def peer(j):
        return lax.rem(me + j, groups)

    barrier = pltpu.get_barrier_semaphore()
    for j in range(1, groups):
        pl.semaphore_signal(barrier, inc=1, device_id={"member": peer(j)}, device_id_type=MESH)

    @pl.when(reg > 0)
    def _():
        pl.semaphore_signal(barrier, inc=1, device_id={"region": reg - 1}, device_id_type=MESH)

    @pl.when(reg < regions - 1)
    def _():
        pl.semaphore_signal(barrier, inc=1, device_id={"region": reg + 1}, device_id_type=MESH)

    own_copies = [
        pltpu.make_async_copy(
            prior, yall.at[pl.ds(pl.multiple_of(me * rows, rows), rows), pl.ds(RIM, obs)], loc_sem.at[0]
        ),
        pltpu.make_async_copy(value, vw.at[pl.ds(rim_rows, obs_rows), :], loc_sem.at[1]),
        pltpu.make_async_copy(rinv, rw.at[pl.ds(rim_rows, obs_rows), :], loc_sem.at[2]),
        pltpu.make_async_copy(tobs, tv, loc_sem.at[4]),
        pltpu.make_async_copy(tcount, ts, loc_sem.at[5]),
    ]
    for copy in own_copies:
        copy.start()

    def state_copy(p, j, t, source):
        return pltpu.make_async_remote_copy(
            src_ref=state.at[:, pl.ds(pl.multiple_of(p * block + t * cells, 128), cells)],
            dst_ref=xall.at[pl.ds(pl.multiple_of(me * rows, rows), rows), pl.ds(t * cells, cells)],
            send_sem=ss_sem.at[j, t],
            recv_sem=sr_sem.at[source, t],
            device_id={"member": p},
            device_id_type=MESH,
        )

    def partner(j):
        flips = []
        for bit in range(max(chips - 1, 1).bit_length()):
            size = 2**bit
            flips.append(size * (1 - 2 * lax.rem(chip // size, 2)))
        if j in (1, 2) and chips > 2:
            one, two = (flips[0], flips[1]) if j == 1 else (flips[1], flips[0])
            return chip + one * (1 - core) + two * core
        return chip + sum(flips[bit] for bit in range(len(flips)) if j >> bit & 1)

    def across(j):
        return partner(j) * CORES + core, CORES * j

    own_state = pltpu.make_async_copy(
        state.at[:, pl.ds(pl.multiple_of(me * block, 128), block)],
        xall.at[pl.ds(pl.multiple_of(me * rows, rows), rows), :],
        loc_sem.at[3],
    )
    own_state.start()

    @pl.when(reg == 0)
    def _():
        yall[:, :RIM] = jnp.zeros((members, RIM), BF16)
        vw[:rim_rows, :] = jnp.zeros((rim_rows, 128), F32)
        rw[:rim_rows, :] = jnp.zeros((rim_rows, 128), F32)

    @pl.when(reg == regions - 1)
    def _():
        yall[:, RIM + obs :] = jnp.zeros((members, RIM), BF16)
        vw[rim_rows + obs_rows :, :] = jnp.zeros((rim_rows, 128), F32)
        rw[rim_rows + obs_rows :, :] = jnp.zeros((rim_rows, 128), F32)

    expected = groups - 1 + (reg > 0).astype(jnp.int32) + (reg < regions - 1).astype(jnp.int32)
    pl.semaphore_wait(barrier, expected)

    def halo(side):
        at = reg - 1 if side == 0 else reg + 1
        src, dst = (0, RIM + obs) if side == 0 else (obs - RIM, 0)
        src_row, dst_row = src // 128, dst // 128
        made = []
        for n, (a, b) in enumerate(
            (
                (value.at[pl.ds(src_row, rim_rows), :], vw.at[pl.ds(dst_row, rim_rows), :]),
                (rinv.at[pl.ds(src_row, rim_rows), :], rw.at[pl.ds(dst_row, rim_rows), :]),
            )
        ):
            made.append(
                pltpu.make_async_remote_copy(
                    src_ref=a,
                    dst_ref=b,
                    send_sem=hs_sem.at[2 * side + n],
                    recv_sem=hr_sem.at[2 * side + n],
                    device_id={"region": at},
                    device_id_type=MESH,
                )
            )
        return made

    @pl.when(reg > 0)
    def _():
        for copy in halo(0):
            copy.start()

    @pl.when(reg < regions - 1)
    def _():
        for copy in halo(1):
            copy.start()

    bits = (chips - 1).bit_length()
    orders = (list(range(bits)), list(range(bits))[::-1])
    upper = (2 * chip) // chips
    to_region = reg + 1 - 2 * upper
    from_region = reg - 1 + 2 * upper
    can_send = jnp.logical_and(to_region >= 0, to_region < regions)
    can_receive = jnp.logical_and(from_region >= 0, from_region < regions)

    def flipped(mask):
        return chip + sum(
            2**bit * (1 - 2 * lax.rem(chip // 2**bit, 2)) for bit in range(bits) if mask >> bit & 1
        )

    def member(mask):
        return flipped(mask) * CORES + core

    def yblock(m, part):
        if part < 2:
            columns = pl.ds(RIM + part * (obs // 2), obs // 2)
        else:
            columns = pl.ds(pl.multiple_of(upper * (RIM + obs), 128), RIM)
        return yall.at[pl.ds(pl.multiple_of(m * rows, rows), rows), columns]

    def prior_copy(m, part, send_sem, device):
        return pltpu.make_async_remote_copy(
            src_ref=yblock(m, part),
            dst_ref=yblock(m, part),
            send_sem=send_sem,
            recv_sem=yr_sem.at[m, part],
            device_id=device,
            device_id_type=MESH,
        )

    def stage_copies(half, stage):
        flip = 1 << orders[half][stage]
        made = []
        for mask in range(chips):
            if not any(mask >> bit & 1 for bit in orders[half][stage:]):
                made.append(prior_copy(member(mask), half, ys_sem.at[mask ^ flip, half], {"member": member(flip)}))
        return made

    def stage_masks(half, stage):
        flip = 1 << orders[half][stage]
        return [
            mask for mask in range(chips)
            if mask & flip and not any(mask >> bit & 1 for bit in orders[half][stage + 1 :])
        ]

    def forward_copy(mask, part):
        return prior_copy(member(mask), part, fs_sem.at[mask, part], {"member": sibling})

    def plane_copy(mask):
        source = pl.ds(pl.multiple_of(obs + upper * (RIM - obs), 128), RIM)
        m = member(mask)
        return pltpu.make_async_remote_copy(
            src_ref=yall.at[pl.ds(pl.multiple_of(m * rows, rows), rows), source],
            dst_ref=yblock(m, 2),
            send_sem=zs_sem.at[mask],
            recv_sem=yr_sem.at[m, 2],
            device_id={"region": to_region},
            device_id_type=MESH,
        )

    def arrived(half, mask):
        @pl.when(jnp.logical_and(can_send, upper == 1 - half))
        def _():
            plane_copy(mask).start()

        forward_copy(mask, half).start()

    def receive(half, stage):
        for mask in stage_masks(half, stage):
            forward_copy(mask, half).wait_recv()

    def gathered():
        for m in range(chips):
            for half in range(2):
                forward_copy_from(m, half).wait_recv()

    def forward_copy_from(c, part):
        return prior_copy(c * CORES + (CORES - 1 - core), part, fs_sem.at[0, part], {"member": sibling})

    def begin(c, half):
        inner = 1 - (2 * c) // chips
        return (inner if half == 0 else 1 - inner) * half_width

    def other(j):
        return partner(j) * CORES + (CORES - 1 - core), CORES * j + 1

    def others():
        return [make(j) for j in range(1, chips) for make in (across, other)]

    early_state = [make(j) for make in (across, other) for j in range(1, min(chips, 3))]

    def start_state(t):
        for p, far in others():
            if t > 0 or far not in [place for _, place in early_state]:
                state_copy(p, far, t, me).start()

    for copy in own_copies:
        copy.wait()
    for half in range(2):
        for copy in stage_copies(half, 0):
            copy.start()
    for half in range(2):
        arrived(half, 0)
    for p, far in early_state[: len(early_state) // 2]:
        state_copy(p, far, 0, me).start()
    for t in range(per_dev):
        state_copy(sibling, 0, t, me).start()
    for stage in range(1, bits):
        for half in range(2):
            receive(half, stage - 1)
            for copy in stage_copies(half, stage):
                copy.start()
            for mask in stage_masks(half, stage - 1):
                arrived(half, mask)
    for p, far in early_state[len(early_state) // 2 :]:
        state_copy(p, far, 0, me).start()

    @pl.when(reg < regions - 1)
    def _():
        for copy in halo(0):
            copy.wait_recv()

    @pl.when(reg > 0)
    def _():
        for copy in halo(1):
            copy.wait_recv()

    pos0 = chip * (CORES * per_dev * OBS_TILE)
    nrow = width_chip // 128
    hpad = (nrow + 15) // 16 * 16
    slots = tobs.shape[1]
    first = me * per_dev
    lane = lax.broadcasted_iota(jnp.int32, (1, slots), 1)
    hi_iota = lax.broadcasted_iota(jnp.int32, (hpad, slots), 0)
    lo_iota = lax.broadcasted_iota(jnp.int32, (128, slots), 0)
    base = chip * (CORES * per_dev * OBS_TILE // 128)
    values[...] = jnp.concatenate([vw[pl.ds(base + h, 1), :] for h in range(nrow)], axis=1)
    rinv_row = jnp.concatenate([rw[pl.ds(base + h, 1), :] for h in range(nrow)], axis=1)
    place = lax.broadcasted_iota(jnp.int32, (1, width_chip), 1)
    centre0 = RIM + OBS_TILE // 2 + core * (per_dev * OBS_TILE)
    for t in range(per_dev):
        rel = tv[pl.ds(first + t, 1), :] - pos0
        live = lane < ts[first + t]
        hi = jnp.where(live, rel // 128, -1)
        lo = lax.rem(rel, 128)
        one_hi = jnp.where(hi_iota == hi, 1.0, 0.0).astype(BF16)
        one_lo = jnp.where(lo_iota == lo, 1.0, 0.0).astype(BF16)
        grid = mm_nt(one_hi, one_lo)
        mask = jnp.concatenate([grid[h : h + 1, :] for h in range(nrow)], axis=1)
        dist = jnp.abs(place - (centre0 + t * OBS_TILE)).astype(F32) / LOC
        roots[t] = jnp.sqrt(mask * rinv_row / (1.0 + dist * dist))

    chunk = 256
    tiles = range(per_dev)

    def perturb(half):
        for k in range(half_width // chunk):
            at = pl.ds(pl.multiple_of(begin(chip, half) + k * chunk, 128), chunk)
            y = yall[:, pl.ds(pl.multiple_of(pos0 + begin(chip, half) + k * chunk, 128), chunk)].astype(F32)
            ybar = jnp.sum(y, axis=0, keepdims=True) * (1.0 / members)
            pert = y - ybar
            dep = values[:, at] - ybar
            for t in tiles:
                root = roots[t, :, at]
                high, low = split(pert * root)
                uh[t, :members, at] = high
                ul[t, :, at] = low
                scaled = jnp.broadcast_to(root * dep, (8, chunk))
                rough = scaled.astype(BF16).astype(F32)
                uh[t, members:, at] = jnp.concatenate([rough, scaled - rough], axis=0).astype(BF16)

    def products(t, half):
        at = pl.ds(pl.multiple_of(begin(chip, half), 128), half_width)
        both = uh[t, :, at]
        return mm_nt(both, both[:members]), mm_nt(both, ul[t, :, at])

    for half in range(2):
        receive(half, bits - 1)
        for mask in stage_masks(half, bits - 1):
            arrived(half, mask)
    start_state(0)
    gathered()
    perturb(0)

    @pl.when(can_receive)
    def _():
        for mask in range(chips):
            forward_copy(mask, 2).wait_recv()
            forward_copy(mask, 2).start()

    for t in range(1, per_dev):
        start_state(t)
    early = [products(t, 0) for t in tiles]

    @pl.when(can_receive)
    def _():
        for c in range(chips):
            forward_copy_from(c, 2).wait_recv()

    perturb(1)

    row_i = lax.broadcasted_iota(jnp.int32, (members, members), 0)
    col_i = lax.broadcasted_iota(jnp.int32, (members, members), 1)
    eye = jnp.where(row_i == col_i, 1.0, 0.0).astype(F32)
    cs = factors(members)

    def transform(t, between):
        late = products(t, 1)
        main, cross = early[t][0] + late[0], early[t][1] + late[1]
        half = cross[:members]
        amat = (members - 1.0) * eye + main[:members] + (half + half.T)
        mmat = amat * (1.0 / (members - 1.0))
        scale = jnp.sqrt(jnp.sum(jnp.sum(mmat * mmat, axis=0, keepdims=True), axis=1, keepdims=True))
        rhs = main[members : members + 1] + main[members + 8 : members + 9] + cross[members : members + 1]
        p = mmat / scale
        v = jnp.broadcast_to(rhs * (float(np.prod(cs)) / (members - 1.0)) / scale, (16, members))
        e = eye - cs[0] * p
        z = 1.5 * eye - 0.5 * p
        for level in range(max(len(cs), 2 * ITERS - 1)):
            if level < len(cs):
                e2, v2 = split(e), split(v)
            if level < len(cs) - 1:
                both = dot3(tuple(jnp.concatenate(x, axis=0) for x in zip(e2, v2)), e2)
                v = v + both[members:]
                e = (1.0 - cs[level + 1]) * eye + cs[level + 1] * both[:members]
            elif level == len(cs) - 1:
                v = v + dot3(v2, e2)
            if level < 2 * ITERS - 2:
                if level % 2 == 0:
                    p2 = split(p)
                    square = dot3(p2, p2)
                else:
                    p = 2.25 * p + dot3(split(square), split(0.25 * p - 1.5 * eye))
            if level >= 2 and level % 2 == 0 and level <= 2 * ITERS - 2:
                z = dot3(split(z), split(1.5 * eye - 0.5 * p))
            for work in between.get(level, ()):
                work()
        wt[t] = (z / jnp.sqrt(scale) + v[:1]).astype(BF16)

    def result_copy(p, j, n, source):
        return pltpu.make_async_remote_copy(
            src_ref=res.at[pl.ds(pl.multiple_of(p * rows, rows), rows), pl.ds(n * PIECE, PIECE)],
            dst_ref=out.at[:, pl.ds(pl.multiple_of(me * block + n * PIECE, 128), PIECE)],
            send_sem=os_sem.at[j, n],
            recv_sem=or_sem.at[source, n],
            device_id={"member": p},
            device_id_type=MESH,
        )

    def own_result(n):
        return pltpu.make_async_copy(
            res.at[pl.ds(pl.multiple_of(me * rows, rows), rows), pl.ds(n * PIECE, PIECE)],
            out.at[:, pl.ds(pl.multiple_of(me * block + n * PIECE, 128), PIECE)],
            own_sem.at[n],
        )

    pieces = block // PIECE
    tile_pieces = cells // PIECE

    def analysis(n):
        for k in range(PIECE // chunk):
            at = slice(n * PIECE + k * chunk, n * PIECE + (k + 1) * chunk)
            x = xall[:, at].astype(F32)
            xbar = jnp.sum(x, axis=0, keepdims=True) * (1.0 / members)
            pert = (x - xbar).astype(BF16)
            res[:, at] = (xbar + mm(wt[n // tile_pieces], pert)).astype(BF16)
        for p, far in others() + [(sibling, 0)]:
            result_copy(p, far, n, me).start()
        own_result(n).start()

    waiting = {}
    for t in range(per_dev):
        transform(t, waiting)
        if t == 0:
            own_state.wait()
        for j in range(1, groups):
            p = peer(j)
            state_copy(p, j, t, p).wait_recv()
        first_piece = t * tile_pieces
        analysis(first_piece)
        later = range(first_piece + 1, first_piece + tile_pieces)
        if t == per_dev - 1:
            for n in later:
                analysis(n)
        else:
            waiting = {1 + 3 * i: [functools.partial(analysis, n)] for i, n in enumerate(later)}

    for n in range(pieces):
        own_result(n).wait()
        for j in range(1, groups):
            p = peer(j)
            result_copy(p, j, n, p).wait_recv()
        for p, far in [(sibling, 0)] + others():
            result_copy(p, far, n, me).wait_send()
    for t in range(per_dev):
        state_copy(sibling, 0, t, me).wait_send()
        for p, far in others():
            state_copy(p, far, t, me).wait_send()
    for half in range(2):
        for stage in range(bits):
            for copy in stage_copies(half, stage):
                copy.wait_send()
        for mask in range(chips):
            forward_copy(mask, half).wait_send()

    @pl.when(can_send)
    def _():
        for mask in range(chips):
            plane_copy(mask).wait_send()

    @pl.when(can_receive)
    def _():
        for mask in range(chips):
            forward_copy(mask, 2).wait_send()

    @pl.when(reg > 0)
    def _():
        for copy in halo(0):
            copy.wait_send()

    @pl.when(reg < regions - 1)
    def _():
        for copy in halo(1):
            copy.wait_send()


def body(groups, regions, state_prior, obs_prior, obs_value, obs_rinv, tile_obs, tile_count):
    rows = state_prior.shape[0]
    tiles = tile_obs.shape[0]
    per_dev = tiles // groups
    cells = state_prior.shape[1] // tiles
    obs = obs_prior.shape[1]
    members = groups * rows
    chips = groups // CORES
    width_chip = obs + 2 * RIM - (chips - 1) * CORES * per_dev * OBS_TILE
    pieces = per_dev * cells // PIECE
    sizes = (groups, regions, rows, per_dev, cells, obs)
    dma = pltpu.SemaphoreType.DMA
    return pl.pallas_call(
        functools.partial(kernel, sizes),
        out_shape=pltpu.VMEM(state_prior.shape, state_prior.dtype),
        in_specs=[pl.BlockSpec(memory_space=pl.ANY)] * 6,
        out_specs=pl.BlockSpec(memory_space=pltpu.VMEM),
        scratch_shapes=[
            pltpu.VMEM(((obs + 2 * RIM) // 128, 128), F32),
            pltpu.VMEM(((obs + 2 * RIM) // 128, 128), F32),
            pltpu.VMEM(tile_obs.shape, jnp.int32),
            pltpu.SMEM(tile_count.shape, jnp.int32),
            pltpu.VMEM((per_dev, 1, width_chip), F32),
            pltpu.VMEM((1, width_chip), F32),
            pltpu.VMEM((members, obs + 2 * RIM), BF16),
            pltpu.VMEM((members, per_dev * cells), BF16),
            pltpu.VMEM((members, per_dev * cells), BF16),
            pltpu.VMEM((per_dev, members + 16, width_chip), BF16),
            pltpu.VMEM((per_dev, members, width_chip), BF16),
            pltpu.VMEM((per_dev, members, members), BF16),
            dma((8,)),
            dma((pieces,)),
            dma((4,)),
            dma((4,)),
            dma((chips, 2)),
            dma((groups, 3)),
            dma((chips, 3)),
            dma((chips,)),
            dma((groups, per_dev)),
            dma((groups, per_dev)),
            dma((groups, pieces)),
            dma((groups, pieces)),
        ],
        compiler_params=pltpu.CompilerParams(
            collective_id=0, has_side_effects=True, vmem_limit_bytes=57 * 1024 * 1024
        ),
        cost_estimate=pl.CostEstimate(flops=4_000_000_000, bytes_accessed=8_000_000, transcendentals=0),
    )(
        state_prior,
        obs_prior,
        obs_value.reshape(-1, 128),
        obs_rinv.reshape(-1, 128),
        tile_obs,
        tile_count,
    )


def solution(mesh):
    placed = (
        P("member", "region"),
        P("member", "region"),
        P("region"),
        P("region"),
        P("region", None),
        P("region"),
    )
    return jax.shard_map(
        functools.partial(body, mesh.shape["member"], mesh.shape["region"]),
        mesh=mesh,
        in_specs=placed,
        out_specs=P("member", "region"),
        check_vma=False,
    )
```
